32 devices in a mesh: pipe: 2 (over core), dp: 4 (over z), tensor: 4 (over y, x).
Axes of the slice: x: 2, y: 2, z: 4, core: 2. Of those that a mesh axis runs over, the one named last changes fastest.
Arguments:
- peak_data: bfloat16 [8192, 100352], P('dp', 'tensor'), may hold values from 0 to 1, as said below
- region_weights: bfloat16 [2, 100352, 128], P('pipe', 'tensor'), may hold values from -0.35355339 to 0.35355339
- out_bias: float32 [100352], P('tensor'), may hold values from -4 to 4
- region_factor: float32 [100352], P('tensor'), may hold values from 0.3 to 0.95
- region_keep: int32 [100352], P('tensor'), may hold values 0 or 1
- cell_factor: float32 [8192], P('dp'), may hold values from 0.3 to 0.95
- batch_ids: int32 [8192], P('dp'), may hold values from 0 to 9
- latent_noise: float32 [8192, 10], P('dp'), may hold values from -4 to 4
- enc_bias_in: float32 [128], replicated, may hold values from -3 to 3
- enc_square: float32 [128, 128], replicated, may hold values from -0.5 to 0.5
- enc_bias_two: float32 [128], replicated, may hold values from -3 to 3
- enc_heads: float32 [128, 20], replicated, may hold values from -0.5 to 0.5
- head_bias: float32 [20], replicated, may hold values from -3 to 3
- dec_first: float32 [20, 128], replicated, may hold values from -2 to 2
- dec_bias_one: float32 [128], replicated, may hold values from -3 to 3
- dec_square: float32 [128, 128], replicated, may hold values from -0.5 to 0.5
- dec_bias_two: float32 [128], replicated, may hold values from -3 to 3
Outputs:
- region_grad: float32 [2, 100352, 128], P('pipe', 'tensor', 'dp')
- out_bias_grad: float32 [100352], P('tensor')
- enc_bias_in_grad: float32 [128], replicated
- enc_square_grad: float32 [128, 128], replicated
- enc_bias_two_grad: float32 [128], replicated
- enc_heads_grad: float32 [128, 20], replicated
- head_bias_grad: float32 [20], replicated
- dec_first_grad: float32 [20, 128], replicated
- dec_bias_one_grad: float32 [128], replicated
- dec_square_grad: float32 [128, 128], replicated
- dec_bias_two_grad: float32 [128], replicated
- mean_loss: float32 [], replicated
The draws below stay inside these ranges and needn't reach their ends.
Inputs may be any that keep to these rules, and one draw needn't show every extreme that they name: `peak_data`: each entry is 0 or 1.
All inputs are finite; a program needn't handle non-finite values. No bound on the sum of `region_keep` on one device may be relied on, other than what follows from the above.
Results may differ from the reference program's by a relative error of at most 0.00059.
Values may be sent and summed in bfloat16 or wider, within the bound.
No kernel may reach another device: no remote copies, remote signals or barrier semaphores. Data moves between devices by JAX's collectives and lax.ppermute only.
A program may use at most 384 MiB of HBM per device.

```python
import jax
import jax.numpy as jnp
from jax import lax

R = 100352
H = 128
L = 10
NB = 10
CELL_DEV = 2048
MB = 4
CELLS = 8192


def draw_peak_data(key, part):
    key = jax.random.fold_in(key, 11)
    rate_key, depth_key, cell_key = jax.random.split(key, 3)
    region_rates = jnp.exp(jax.random.uniform(rate_key, (R,), jnp.float32, jnp.log(0.04), jnp.log(0.6)))
    depths = jnp.exp(jax.random.uniform(depth_key, (CELLS, 1), jnp.float32, jnp.log(0.5), jnp.log(1.5)))
    chances = jax.random.uniform(cell_key, (CELLS, R), jnp.float32)
    return (chances < region_rates[None, :] * depths).astype(jnp.float32).astype(jnp.bfloat16)


def draw_region_weights(key, part):
    key = jax.random.fold_in(key, 23)
    values = jax.random.truncated_normal(key, -4.0, 4.0, (2, R, H), jnp.float32)
    section_scale = jnp.where(jnp.arange(2)[:, None, None] == 0, (R / 5.0) ** (-0.5), H ** (-0.5))
    return (values * section_scale).astype(jnp.bfloat16)


def with_ends(drawn, rng, smallest, top_value):
    shape = drawn.shape
    place = [jax.random.randint(jax.random.fold_in(rng, axis), (), 0, shape[axis]) for axis in range(len(shape))]
    drawn = drawn.at[tuple(place)].set(smallest)
    longest = shape.index(max(shape))
    place[longest] = (place[longest] + 1) % shape[longest]
    return drawn.at[tuple(place)].set(top_value)


def levels(stream_key, shape, shards, smallest, largest):
    factor_of, own = 1.0, jax.random.fold_in(stream_key, 6)
    for axis_at, blocks in shards:
        heights = jnp.exp(jax.random.uniform(jax.random.fold_in(own, axis_at), (blocks,), jnp.float32, smallest / len(shards), largest / len(shards)))
        factor_of = factor_of * jnp.repeat(heights, shape[axis_at] // blocks).reshape([-1 if axis == axis_at else 1 for axis in range(len(shape))])
    return factor_of


def gaussian(key, shape, spread, reach, pieces=(), kind=jnp.bfloat16):
    drawn = spread * jax.random.normal(key, shape, jnp.float32)
    if pieces:
        drawn = drawn * levels(key, shape, pieces, -0.22, 0.18)
    return jnp.clip(drawn, -reach, reach).astype(kind)


def setup_inputs(seed: int = 0) -> dict:
    key_list = jax.random.split(jax.random.key(seed), 18)
    peak_data = draw_peak_data(jax.random.fold_in(key_list[17], 71), 0)
    region_weights = draw_region_weights(jax.random.fold_in(key_list[17], 71), 0)
    out_bias = gaussian(key_list[2], (R,), 1.0, 4.0, ((0, 4),), jnp.float32)
    region_factor = jnp.clip(0.3 + 0.65 * jax.random.uniform(key_list[3], (R,), jnp.float32) ** levels(key_list[3], (R,), ((0, 4),), -0.2, 0.2), 0.3, 0.95)
    region_keep = with_ends((jax.random.randint(key_list[4], (R,), 0, 8) < 7).astype(jnp.int32), jax.random.fold_in(key_list[4], 1), 0, 1)
    cell_factor = jnp.clip(0.3 + 0.65 * jax.random.uniform(key_list[5], (CELLS,), jnp.float32) ** levels(key_list[5], (CELLS,), ((0, 4),), -0.2, 0.2), 0.3, 0.95)
    batch_ids = with_ends(jax.random.randint(key_list[6], (CELLS,), 0, NB), jax.random.fold_in(key_list[6], 1), 0, NB - 1).astype(jnp.int32)
    latent_noise = gaussian(key_list[7], (CELLS, L), 1.0, 4.0, ((0, 4),), jnp.float32)
    enc_bias_in = gaussian(key_list[8], (H,), 0.5, 3.0, (), jnp.float32)
    enc_square = gaussian(key_list[9], (H, H), H ** -0.5, 0.5, (), jnp.float32)
    enc_bias_two = gaussian(key_list[10], (H,), 0.5, 3.0, (), jnp.float32)
    enc_heads = gaussian(key_list[11], (H, 2 * L), H ** -0.5, 0.5, (), jnp.float32)
    head_bias = gaussian(key_list[12], (2 * L,), 0.5, 3.0, (), jnp.float32)
    dec_first = gaussian(key_list[13], (L + NB, H), L ** -0.5, 2.0, (), jnp.float32)
    dec_bias_one = gaussian(key_list[14], (H,), 0.5, 3.0, (), jnp.float32)
    dec_square = gaussian(key_list[15], (H, H), H ** -0.5, 0.5, (), jnp.float32)
    dec_bias_two = gaussian(key_list[16], (H,), 0.5, 3.0, (), jnp.float32)
    return dict(peak_data=peak_data, region_weights=region_weights, out_bias=out_bias, region_factor=region_factor, region_keep=region_keep, cell_factor=cell_factor, batch_ids=batch_ids, latent_noise=latent_noise, enc_bias_in=enc_bias_in, enc_square=enc_square, enc_bias_two=enc_bias_two, enc_heads=enc_heads, head_bias=head_bias, dec_first=dec_first, dec_bias_one=dec_bias_one, dec_square=dec_square, dec_bias_two=dec_bias_two)


EXACT = lax.Precision.HIGHEST
NORM_EPS = 1e-05

@jax.custom_vjp
def low(v):
    return lax.optimization_barrier(v.astype(jnp.bfloat16)).astype(jnp.float32)

@jax.custom_vjp
def low_back(v):
    return v

def low_keep(v):
    return (low(v), None)

def low_pass(kept, grad):
    return (grad,)

def back_keep(v):
    return (v, None)

def back_low(kept, grad):
    return (low(grad),)
low.defvjp(low_keep, low_pass)
low_back.defvjp(back_keep, back_low)

def layer_norm(values):
    centred = values - lax.optimization_barrier(jnp.mean(values, axis=-1, keepdims=True))
    return centred * lax.rsqrt(lax.optimization_barrier(jnp.mean(centred * centred, axis=-1, keepdims=True)) + NORM_EPS)

def encoder_small(summed, bias_in, square, bias_two, head_w, head_bias, noise_rows):
    hidden = jax.nn.silu(layer_norm(summed + bias_in))
    hidden = jax.nn.silu(layer_norm(jnp.dot(hidden, square, precision=EXACT) + bias_two))
    head_out = jnp.dot(hidden, head_w, precision=EXACT) + head_bias
    latent = noise_rows.shape[1]
    average = head_out[:, :latent]
    variance = jnp.exp(head_out[:, latent:]) + 0.0001
    sample = average + jnp.sqrt(variance) * noise_rows
    kl_sum = 0.5 * jnp.sum(average * average + variance - jnp.log(variance) - 1.0)
    return (sample, kl_sum)

def decoder_small(inputs, first_w, bias_one, square, bias_two):
    hidden = jax.nn.silu(layer_norm(jnp.dot(inputs, first_w, precision=EXACT) + bias_one))
    return jax.nn.silu(layer_norm(jnp.dot(hidden, square, precision=EXACT) + bias_two))

def region_loss(logit, peak_rows, keep_mask, region_factor, cell_rows):
    factor = region_factor[None, :] * cell_rows[:, None]
    chance = jax.nn.sigmoid(logit)
    log_prob = jax.nn.log_sigmoid(logit) + jnp.log(factor)
    log_rest = jnp.log1p(-chance * factor)
    return -jnp.sum(keep_mask[None, :] * (peak_rows * log_prob + (1.0 - peak_rows) * log_rest))

def reference(peak_data, region_weights, out_bias, region_factor, region_keep, cell_factor, batch_ids, latent_noise, enc_bias_in, enc_square, enc_bias_two, enc_heads, head_bias, dec_first, dec_bias_one, dec_square, dec_bias_two):
    block_rows = CELL_DEV // MB
    blocks = CELLS // block_rows
    keep_mask = region_keep.astype(jnp.float32)
    batch_codes = jnp.arange(NB, dtype=jnp.int32)
    onehot = (batch_ids[:, None] == batch_codes[None, :]).astype(jnp.float32)
    items = (peak_data.reshape(blocks, block_rows, R), latent_noise.reshape(blocks, block_rows, L), onehot.reshape(blocks, block_rows, NB), cell_factor.reshape(blocks, block_rows))
    params = (region_weights.astype(jnp.float32), out_bias, enc_bias_in, enc_square, enc_bias_two, enc_heads, head_bias, dec_first, dec_bias_one, dec_square, dec_bias_two)

    def objective(weights, bias_out, bias_in, enc_sq, enc_two, enc_head, enc_hbias, dec_one_w, dec_one_b, dec_sq, dec_two):

        def block_step(running, block_item):
            peak_rows = block_item[0].astype(jnp.float32)
            summed = low_back(jnp.dot(peak_rows, weights[0], precision=EXACT))
            sample, kl_sum = encoder_small(summed, bias_in, enc_sq, enc_two, enc_head, enc_hbias, block_item[1])
            sent = low(low_back(sample))
            hidden = decoder_small(jnp.concatenate([sent, block_item[2]], axis=1), dec_one_w, dec_one_b, dec_sq, dec_two)
            logit = low_back(jnp.dot(low(hidden), weights[1].T, precision=EXACT)) + bias_out
            recon = region_loss(logit, peak_rows, keep_mask, region_factor, block_item[3])
            return (running + recon + kl_sum, None)
        total, unused = lax.scan(jax.checkpoint(block_step), jnp.zeros((), jnp.float32), items)
        return total
    total, pull = jax.vjp(objective, *params)
    pulled = pull(jnp.ones_like(total) * CELLS ** (-0.5))
    mean_loss = total / (CELLS * R)
    return (pulled[0], pulled[1], pulled[2], pulled[3], pulled[4], pulled[5], pulled[6], pulled[7], pulled[8], pulled[9], pulled[10], mean_loss)
```

```python
import functools

import jax
import jax.numpy as jnp
import numpy as np
from jax import lax
from jax.experimental import pallas as pl
from jax.experimental.pallas import tpu as pltpu
from jax.sharding import PartitionSpec as P

EXACT = lax.Precision.HIGHEST
NORM_EPS = 1e-05
LOG2E = float(np.log2(np.e))
LN2 = float(np.log(2.0))
BIG_BITS = 56
BIG = float(2.0**BIG_BITS)
MIB = 1 << 20
EXTRA = 16


def params_of(mib):
    return pltpu.CompilerParams(vmem_limit_bytes=mib * MIB)


def layer_norm(values):
    centred = values - jnp.mean(values, axis=-1, keepdims=True)
    return centred * lax.rsqrt(jnp.mean(centred * centred, axis=-1, keepdims=True) + NORM_EPS)


def silu(values):
    return values * jax.nn.sigmoid(values)


def mm(a, b):
    return lax.dot_general(a, b, (((1,), (0,)), ((), ())), precision=EXACT, preferred_element_type=jnp.float32)


def encoder_small(summed, bias_in, square, bias_two, mean_w, var_w, mean_b, var_b, noise_rows):
    hidden = silu(layer_norm(summed + bias_in))
    hidden = silu(layer_norm(mm(hidden, square) + bias_two))
    average = mm(hidden, mean_w) + mean_b
    variance = jnp.exp(mm(hidden, var_w) + var_b) + 0.0001
    sample = average + jnp.sqrt(variance) * noise_rows
    kl_rows = 0.5 * jnp.sum(average * average + variance - jnp.log(variance) - 1.0, axis=1, keepdims=True)
    return (sample, jnp.sum(kl_rows, axis=0, keepdims=True))


def decoder_small(latent_rows, onehot, first_z, first_b, bias_one, square, bias_two):
    hidden = silu(layer_norm(mm(latent_rows, first_z) + mm(onehot, first_b) + bias_one))
    return silu(layer_norm(mm(hidden, square) + bias_two))


def onehot_of(ids, width):
    codes = lax.broadcasted_iota(jnp.int32, (ids.shape[0], width), 1)
    return (ids == codes).astype(jnp.float32)


def forward_kernel(count, *refs):
    parts = refs[:count]
    noise, ids = refs[count : count + 2]
    enc = [r[...] for r in refs[count + 2 : count + 9]]
    dec = [r[...] for r in refs[count + 9 : count + 14]]
    summed_out, z_out, g2_out, kl_out = refs[count + 14 :]
    summed = parts[0][...]
    for part in parts[1:]:
        summed = summed + part[...]
    sample, kl_sum = encoder_small(summed, *enc, noise[...])
    z_low = sample.astype(jnp.bfloat16)
    hidden = decoder_small(z_low.astype(jnp.float32), onehot_of(ids[...], dec[1].shape[0]), *dec)
    summed_out[...] = summed
    z_out[...] = z_low
    g2_out[...] = hidden.astype(jnp.bfloat16)
    kl_out[...] = kl_sum


def backward_kernel(count, norm_scale, *refs):
    parts = refs[:count]
    summed, z_low, noise, ids = refs[count : count + 4]
    enc = [r[...] for r in refs[count + 4 : count + 11]]
    dec = [r[...] for r in refs[count + 11 : count + 16]]
    outs = refs[count + 16 :]
    dg2 = parts[0][...]
    for part in parts[1:]:
        dg2 = dg2 + part[...]
    onehot = onehot_of(ids[...], dec[1].shape[0])
    unused, pull = jax.vjp(lambda z, *w: decoder_small(z, onehot, *w), z_low[...].astype(jnp.float32), *dec)
    dz, *dec_grads = pull(dg2)
    noise_rows = noise[...]
    unused, pull = jax.vjp(lambda s, *w: encoder_small(s, *w, noise_rows), summed[...], *enc)
    dz_low = dz.astype(jnp.bfloat16).astype(jnp.float32)
    dp, *enc_grads = pull((dz_low, jnp.full((1, 1), norm_scale, jnp.float32)))
    outs[0][...] = dp.astype(jnp.bfloat16)
    for out, grad in zip(outs[1:], enc_grads + dec_grads):
        out[...] = grad


def project_kernel(half_ref, x_ref, w_ref, out_ref):
    out_ref[...] = jnp.dot(x_ref[...], w_ref[...], preferred_element_type=jnp.float32)


def project(half, peaks, weight):
    cells, width = peaks.shape[0], weight.shape[1]
    regions = weight.shape[0]
    rows = min(256, cells)
    return pl.pallas_call(
        project_kernel,
        grid_spec=pltpu.PrefetchScalarGridSpec(
            num_scalar_prefetch=1,
            grid=(cells // rows,),
            in_specs=[
                pl.BlockSpec((rows, regions), lambda i, h: (i, h[0])),
                pl.BlockSpec((regions, width), lambda i, h: (0, 0)),
            ],
            out_specs=pl.BlockSpec((rows, width), lambda i, h: (i, 0)),
        ),
        out_shape=jax.ShapeDtypeStruct((cells, width), jnp.float32),
        compiler_params=params_of(48),
        cost_estimate=pl.CostEstimate(
            flops=2 * cells * regions * width, bytes_accessed=2 * cells * regions, transcendentals=0
        ),
        name="project",
    )(half, peaks, weight)


def regions_kernel(
    tile, rows_at_once, piece, half_ref, x_ref, w_ref, g_ref, gt_ref, a_ref, fa_ref, ck_ref, cf_ref, before_ref,
    dg_ref, dw_ref, st_ref, m0, m1, e0, e1, g_s,
):
    cells, chunk = x_ref.shape
    blocks = cells // rows_at_once
    M, E = (m0, m1), (e0, e1)

    @pl.when(pl.program_id(0) == 0)
    def first():
        dg_ref[...] = before_ref[...]
        scaled = g_ref[...].astype(jnp.float32) * (-LOG2E)
        high = scaled.astype(jnp.bfloat16)
        g_s[:, :128] = high
        g_s[:, 128:] = (scaled - high.astype(jnp.float32)).astype(jnp.bfloat16)

    def one_tile(t, carry):
        cols = pl.ds(pl.multiple_of(t * tile, 128), tile)
        w = w_ref[cols, :]
        w2 = jnp.concatenate([w, w], axis=1)
        wide = (8, tile)
        a = jnp.broadcast_to(a_ref[:, cols], wide)[None]
        fa = jnp.broadcast_to(fa_ref[:, cols], wide)[None]
        ck = jnp.broadcast_to(ck_ref[:, cols], wide)[None]

        def rows(i, o=0, n=rows_at_once):
            return pl.ds(pl.multiple_of(i * rows_at_once + o, 16), n)

        def logit(i, s, o, n):
            M[s][o : o + n, :] = lax.dot_general(
                g_s[rows(i, o, n), :], w2, (((1,), (1,)), ((), ())), preferred_element_type=jnp.float32
            )

        def elementwise(i, s, o, sums):
            e_sum, l_sum = sums
            shape = (piece // 8, 8, tile)
            u = jnp.exp2(M[s][o : o + piece, :]).reshape(shape)
            cf = cf_ref[rows(i, o, piece), :]
            cf = jnp.concatenate([cf] * (tile // 128), axis=1).reshape(shape)
            seen = (x_ref[rows(i, o, piece), cols] * jnp.bfloat16(BIG)).astype(jnp.float32).reshape(shape)
            total = u + a
            rest = (total - fa * cf) + seen
            d = pltpu.reciprocal(rest, approx=True)
            slope = (u * ck) * (d - pltpu.reciprocal(total, approx=True))
            ratio = (d * total).reshape(piece // 16, 2, 8, tile)
            E[s][o : o + piece, :] = slope.reshape(piece, tile).astype(jnp.bfloat16)
            e_sum = e_sum + jnp.sum(slope, axis=0)
            l_sum = l_sum + jnp.sum(jnp.log2(ratio[:, 0] * ratio[:, 1]), axis=0)
            return e_sum, l_sum

        def cell_grad(i, s):
            dg_ref[rows(i), :] += jnp.dot(E[s][...], w, preferred_element_type=jnp.float32)

        def region_grad(i, s, start=False):
            part = jnp.dot(gt_ref[i], E[s][...], preferred_element_type=jnp.float32)
            if start:
                dw_ref[:, cols] = part
            else:
                dw_ref[:, cols] += part

        def step(i, s, sums, logits=True, grads=True, start=False):
            dots = rows_at_once // 2
            for o in range(0, rows_at_once, piece):
                if logits and o % dots == 0:
                    logit(i + 1, 1 - s, o, dots)
                sums = elementwise(i, s, o, sums)
                if grads and o == dots:
                    cell_grad(i - 1, 1 - s)
            if grads:
                region_grad(i - 1, 1 - s, start)
            return sums

        zero = jnp.zeros(wide, jnp.float32)
        sums = (zero, zero)
        logit(0, 0, 0, rows_at_once)
        sums = step(0, 0, sums, grads=False)
        for i in range(1, blocks):
            sums = step(i, i % 2, sums, logits=i < blocks - 1, start=i == 1)
        cell_grad(blocks - 1, (blocks - 1) % 2)
        region_grad(blocks - 1, (blocks - 1) % 2, blocks == 1)
        st_ref[0:8, cols] = sums[0]
        st_ref[8:16, cols] = sums[1]
        return carry

    lax.fori_loop(0, chunk // tile, one_tile, 0)


def regions_pass(half, peaks, weight, hidden, hidden_t, a, fa, ck, cf, before, first, count, chunk, per_half):
    cells, width = hidden.shape
    tile, rows, piece = min(256, chunk), min(512, cells // 2), 64
    blocks = cells // rows
    return pl.pallas_call(
        functools.partial(regions_kernel, tile, rows, piece),
        grid_spec=pltpu.PrefetchScalarGridSpec(
            num_scalar_prefetch=1,
            grid=(count,),
            in_specs=[
                pl.BlockSpec((cells, chunk), lambda j, h: (0, h[0] * per_half + first + j)),
                pl.BlockSpec((chunk, width), lambda j, h: (first + j, 0)),
                pl.BlockSpec((cells, width), lambda j, h: (0, 0)),
                pl.BlockSpec((blocks, width, rows), lambda j, h: (0, 0, 0)),
                pl.BlockSpec((1, chunk), lambda j, h: (0, first + j)),
                pl.BlockSpec((1, chunk), lambda j, h: (0, first + j)),
                pl.BlockSpec((1, chunk), lambda j, h: (0, first + j)),
                pl.BlockSpec((cells, 128), lambda j, h: (0, 0)),
                pl.BlockSpec((cells, width), lambda j, h: (0, 0)),
            ],
            out_specs=[
                pl.BlockSpec((cells, width), lambda j, h: (0, 0)),
                pl.BlockSpec((width, chunk), lambda j, h: (0, j)),
                pl.BlockSpec((16, chunk), lambda j, h: (0, j)),
            ],
            scratch_shapes=[pltpu.VMEM((rows, tile), jnp.float32)] * 2
            + [pltpu.VMEM((rows, tile), jnp.bfloat16)] * 2
            + [pltpu.VMEM((cells, 2 * width), jnp.bfloat16)],
        ),
        out_shape=[
            jax.ShapeDtypeStruct((cells, width), jnp.float32),
            jax.ShapeDtypeStruct((width, count * chunk), jnp.float32),
            jax.ShapeDtypeStruct((16, count * chunk), jnp.float32),
        ],
        compiler_params=params_of(56),
        cost_estimate=pl.CostEstimate(
            flops=10 * cells * count * chunk * width,
            bytes_accessed=2 * cells * count * chunk,
            transcendentals=16 * cells * count * chunk,
        ),
        name="regions",
    )(half, peaks, weight, hidden, hidden_t, a, fa, ck, cf, before)


def outer_kernel(half_ref, x_ref, t_ref, dw_ref, extra_ref):
    width = dw_ref.shape[0]
    tile = min(256, x_ref.shape[1])
    for c in range(0, x_ref.shape[1], tile):
        part = jnp.dot(t_ref[...], x_ref[:, c : c + tile], preferred_element_type=jnp.float32)
        dw_ref[:, c : c + tile] = part[:width]
        extra_ref[:, c : c + tile] = part[width:]


def outer(half, peaks, left, first, count, chunk, per_half):
    cells = peaks.shape[0]
    width = left.shape[0] - EXTRA
    return pl.pallas_call(
        outer_kernel,
        grid_spec=pltpu.PrefetchScalarGridSpec(
            num_scalar_prefetch=1,
            grid=(count,),
            in_specs=[
                pl.BlockSpec((cells, chunk), lambda j, h: (0, h[0] * per_half + first + j)),
                pl.BlockSpec((width + EXTRA, cells), lambda j, h: (0, 0)),
            ],
            out_specs=[
                pl.BlockSpec((width, chunk), lambda j, h: (0, j)),
                pl.BlockSpec((EXTRA, chunk), lambda j, h: (0, j)),
            ],
        ),
        out_shape=[
            jax.ShapeDtypeStruct((width, count * chunk), jnp.float32),
            jax.ShapeDtypeStruct((EXTRA, count * chunk), jnp.float32),
        ],
        compiler_params=params_of(48),
        cost_estimate=pl.CostEstimate(
            flops=2 * cells * count * chunk * width, bytes_accessed=2 * cells * count * chunk, transcendentals=0
        ),
        name="outer",
    )(half, peaks, left)


def part_of(values, which, size, axis=0):
    return lax.dynamic_slice_in_dim(values, which * size, size, axis)


def across_cores(values):
    return lax.ppermute(values, "pipe", [(0, 1), (1, 0)])


def shift_of(step, index, count):
    if count & (count - 1) == 0:
        return index ^ step
    return (index + step) % count


def scatter_cells(partial):
    cells = partial.shape[0]
    pipe, mine, count = lax.axis_index("pipe"), lax.axis_index("tensor"), lax.axis_size("tensor")
    half = cells // 2
    got = across_cores(part_of(partial, 1 - pipe, half))
    chip_sum = part_of(partial, pipe, half) + got
    rows = half // count
    pieces = [part_of(chip_sum, mine, rows)]
    for step in range(1, count):
        there = shift_of(step, mine, count)
        route = [(i, shift_of(step, i, count)) for i in range(count)]
        pieces.append(lax.ppermute(part_of(chip_sum, there, rows), "tensor", route))
    return pieces


def gather_cells(own):
    pipe, mine, count = lax.axis_index("pipe"), lax.axis_index("tensor"), lax.axis_size("tensor")
    rows = own.shape[0]
    half = jnp.zeros((rows * count, own.shape[1]), own.dtype)
    half = lax.dynamic_update_slice_in_dim(half, own, mine * rows, 0)
    for step in range(1, count):
        route = [(i, shift_of(step, i, count)) for i in range(count)]
        got = lax.ppermute(own, "tensor", route)
        sender = mine ^ step if count & (count - 1) == 0 else (mine - step) % count
        half = lax.dynamic_update_slice_in_dim(half, got, sender * rows, 0)
    other = across_cores(half)
    return jnp.concatenate([jnp.where(pipe == 0, half, other), jnp.where(pipe == 0, other, half)], axis=0)


def three_terms(values):
    high = values.astype(jnp.bfloat16)
    rest = values - high.astype(jnp.float32)
    middle = rest.astype(jnp.bfloat16)
    return high, middle, (rest - middle.astype(jnp.float32)).astype(jnp.bfloat16)


def body(
    peak_data,
    region_weights,
    out_bias,
    region_factor,
    region_keep,
    cell_factor,
    batch_ids,
    latent_noise,
    enc_bias_in,
    enc_square,
    enc_bias_two,
    enc_heads,
    head_bias,
    dec_first,
    dec_bias_one,
    dec_square,
    dec_bias_two,
):
    cells, regions_local = peak_data.shape
    weight = region_weights[0]
    width = weight.shape[1]
    latent = latent_noise.shape[1]
    batches = dec_first.shape[0] - latent
    window = -(-regions_local // 256) * 128
    overlap = 2 * window - regions_local
    pipe, mine, tensors = lax.axis_index("pipe"), lax.axis_index("tensor"), lax.axis_size("tensor")
    cell_total = cells * lax.axis_size("dp")
    region_total = regions_local * tensors
    norm_scale = float(cell_total) ** (-0.5)

    def of_core(values, core, axis=0):
        return lax.dynamic_slice_in_dim(values, core * (regions_local - window), window, axis)

    kept = of_core(weight, pipe)
    got = across_cores(of_core(weight, 1 - pipe))
    w_enc = jnp.where(pipe == 0, kept, got)
    w_dec = jnp.where(pipe == 0, got, kept)
    keep = of_core(region_keep, pipe).astype(jnp.float32)
    half = jnp.reshape(pipe, (1,)).astype(jnp.int32)
    if overlap:
        mine_alone = (pipe == 0) | (jnp.arange(window) >= overlap)
        w_enc = jnp.where(mine_alone[:, None], w_enc, 0)
        keep = jnp.where(mine_alone, keep, 0.0)
        peak_data = of_core(peak_data, pipe, 1)
        half = jnp.zeros_like(half)

    own_rows = cells // (2 * tensors)
    own_at = pipe * tensors + mine
    noise_own = part_of(latent_noise, own_at, own_rows)
    ids_own = part_of(batch_ids[:, None], own_at, own_rows)
    enc = (
        enc_bias_in[None], enc_square, enc_bias_two[None], enc_heads[:, :latent], enc_heads[:, latent:],
        head_bias[None, :latent], head_bias[None, latent:],
    )
    dec = (dec_first[:latent], dec_first[latent:], dec_bias_one[None], dec_square, dec_bias_two[None])

    a = jnp.exp(of_core(out_bias, pipe))
    fa = a * of_core(region_factor, pipe)
    cf_wide = jnp.broadcast_to(cell_factor[:, None], (cells, 128))
    log_cf = jnp.log(cell_factor)

    vmem = pl.BlockSpec(memory_space=pltpu.VMEM)
    partial = project(half, peak_data, w_enc)
    pieces = scatter_cells(partial)
    summed, z_low, g2_own, kl_sum = pl.pallas_call(
        functools.partial(forward_kernel, len(pieces)),
        in_specs=[vmem] * (len(pieces) + 14),
        out_specs=[vmem] * 4,
        out_shape=[
            jax.ShapeDtypeStruct((own_rows, width), jnp.float32),
            jax.ShapeDtypeStruct((own_rows, latent), jnp.bfloat16),
            jax.ShapeDtypeStruct((own_rows, width), jnp.bfloat16),
            jax.ShapeDtypeStruct((1, 1), jnp.float32),
        ],
        compiler_params=params_of(32),
        name="small_forward",
    )(*pieces, noise_own, ids_own, *enc, *dec)
    hidden = gather_cells(g2_own)

    chunk = next(c for c in (1792, 256, 128) if window % c == 0 and (regions_local - window) % c == 0)
    chunks = window // chunk
    rows_b = min(512, cells // 2)
    hidden_t = jnp.transpose(hidden.reshape(cells // rows_b, rows_b, width), (0, 2, 1))
    ck = (keep * norm_scale)[None]
    cuts = [0, 3, 5, chunks] if chunks == 7 else [0, chunks]
    dg2 = jnp.zeros((cells, width), jnp.float32)
    dw_dec, stats = [], []
    for first, end in zip(cuts[:-1], cuts[1:]):
        dg2, dw, st = regions_pass(
            half, peak_data, w_dec, hidden, hidden_t, a[None], fa[None], ck, cf_wide, dg2, first, end - first, chunk, chunks
        )
        dw_dec.append(lax.psum_scatter(dw, "dp", scatter_dimension=0, tiled=True))
        stats.append(st)
    stats = jnp.concatenate(stats, axis=1)

    pieces = scatter_cells(dg2)
    enc_dec = enc + dec
    grads = pl.pallas_call(
        functools.partial(backward_kernel, len(pieces), norm_scale),
        in_specs=[vmem] * (len(pieces) + 16),
        out_specs=[vmem] * (1 + len(enc_dec)),
        out_shape=[jax.ShapeDtypeStruct((own_rows, width), jnp.bfloat16)]
        + [jax.ShapeDtypeStruct(w.shape, jnp.float32) for w in enc_dec],
        compiler_params=params_of(32),
        name="small_backward",
    )(*pieces, summed, z_low, noise_own, ids_own, *enc, *dec)
    dp_low = gather_cells(grads[0])

    ones = jnp.ones((1, cells), jnp.bfloat16)
    logs = [t[None] for t in three_terms(log_cf)]
    left = jnp.concatenate(
        [jnp.transpose(dp_low), ones, *logs, jnp.zeros((EXTRA - 4, cells), jnp.bfloat16)], axis=0
    )
    dw_enc, extra = outer(half, peak_data, left, 0, chunks, chunk, chunks)
    dw_enc = lax.psum_scatter(dw_enc, "dp", scatter_dimension=0, tiled=True)
    dw_dec = jnp.concatenate(dw_dec, axis=1)

    give = jnp.where(pipe == 0, dw_dec, dw_enc)
    hold = jnp.where(pipe == 0, dw_enc, dw_dec)
    taken = across_cores(give)
    region_grad = jnp.concatenate(
        [jnp.where(pipe == 0, hold, taken), jnp.where(pipe == 0, taken, hold)[:, overlap:]], axis=1
    )
    region_grad = jnp.transpose(region_grad)[None]

    bias_half = jnp.sum(stats[:8], axis=0)
    bias_grad = lax.dynamic_update_slice_in_dim(
        jnp.zeros((regions_local,), jnp.float32), bias_half, pipe * (regions_local - window), 0
    )
    bias_grad = lax.psum(bias_grad, ("pipe", "dp"))

    seen, seen_log = extra[0], extra[1] + extra[2] + extra[3]
    per_region = LN2 * jnp.sum(stats[8:], axis=0) + seen * (BIG_BITS * LN2 - jnp.log(fa)) - seen_log
    loss = jnp.sum(keep * per_region) + kl_sum[0, 0]
    small = lax.psum((*grads[1:], loss), ("pipe", "dp", "tensor"))
    (d_bias_in, d_square, d_bias_two, d_mean_w, d_var_w, d_mean_b, d_var_b, d_first_z, d_first_b, d_bias_one, d_dec_square,
     d_dec_bias_two, loss_total) = small
    mean_loss = loss_total / (cell_total * region_total)
    return (
        region_grad,
        bias_grad,
        d_bias_in[0],
        d_square,
        d_bias_two[0],
        jnp.concatenate([d_mean_w, d_var_w], axis=1),
        jnp.concatenate([d_mean_b[0], d_var_b[0]], axis=0),
        jnp.concatenate([d_first_z, d_first_b], axis=0),
        d_bias_one[0],
        d_dec_square,
        d_dec_bias_two[0],
        mean_loss,
    )


def solution(mesh):
    in_specs = (
        P("dp", "tensor"),
        P("pipe", "tensor", None),
        P("tensor"),
        P("tensor"),
        P("tensor"),
        P("dp"),
        P("dp"),
        P("dp", None),
        *[P()] * 9,
    )
    out_specs = (P("pipe", "tensor", "dp"), P("tensor"), *[P()] * 10)
    return jax.shard_map(body, mesh=mesh, in_specs=in_specs, out_specs=out_specs, check_vma=False)
```

```python
import functools

import jax
import jax.numpy as jnp
import numpy as np
from jax import lax
from jax.experimental import pallas as pl
from jax.experimental.pallas import tpu as pltpu
from jax.sharding import PartitionSpec as P

EXACT = lax.Precision.HIGHEST
NORM_EPS = 1e-05
LOG2E = float(np.log2(np.e))
LN2 = float(np.log(2.0))
BIG_BITS = 56
BIG = float(2.0**BIG_BITS)
MIB = 1 << 20
EXTRA = 16


def params_of(mib):
    return pltpu.CompilerParams(vmem_limit_bytes=mib * MIB)


def layer_norm(values):
    centred = values - jnp.mean(values, axis=-1, keepdims=True)
    return centred * lax.rsqrt(jnp.mean(centred * centred, axis=-1, keepdims=True) + NORM_EPS)


def silu(values):
    return values * jax.nn.sigmoid(values)


def mm(a, b):
    return lax.dot_general(a, b, (((1,), (0,)), ((), ())), precision=EXACT, preferred_element_type=jnp.float32)


def mm_t(a, b):
    return lax.dot_general(a, b, (((1,), (1,)), ((), ())), precision=EXACT, preferred_element_type=jnp.float32)


def encoder_small(summed, bias_in, square, bias_two, mean_w, var_w, mean_b, var_b, noise_rows):
    hidden = silu(layer_norm(summed + bias_in))
    hidden = silu(layer_norm(mm(hidden, square) + bias_two))
    average = mm_t(hidden, mean_w) + mean_b
    variance = jnp.exp(mm_t(hidden, var_w) + var_b) + 0.0001
    sample = average + jnp.sqrt(variance) * noise_rows
    kl_rows = 0.5 * jnp.sum(average * average + variance - jnp.log(variance) - 1.0, axis=1, keepdims=True)
    return (sample, jnp.sum(kl_rows, axis=0, keepdims=True))


def decoder_small(latent_rows, onehot, first_z, first_b, bias_one, square, bias_two):
    hidden = silu(layer_norm(mm(latent_rows, first_z) + mm(onehot, first_b) + bias_one))
    return silu(layer_norm(mm(hidden, square) + bias_two))


def onehot_of(ids, width):
    codes = lax.broadcasted_iota(jnp.int32, (ids.shape[0], width), 1)
    return (ids == codes).astype(jnp.float32)


def forward_kernel(count, *refs):
    parts = refs[:count]
    noise, ids = refs[count : count + 2]
    enc = [r[...] for r in refs[count + 2 : count + 9]]
    dec = [r[...] for r in refs[count + 9 : count + 14]]
    summed_out, z_out, g2_out, kl_out = refs[count + 14 :]
    summed = parts[0][...]
    for part in parts[1:]:
        summed = summed + part[...]
    sample, kl_sum = encoder_small(summed, *enc, noise[...])
    z_low = sample.astype(jnp.bfloat16)
    hidden = decoder_small(z_low.astype(jnp.float32), onehot_of(ids[...], dec[1].shape[0]), *dec)
    summed_out[...] = summed
    z_out[...] = z_low
    g2_out[...] = hidden.astype(jnp.bfloat16)
    kl_out[...] = kl_sum


def pack_places(shapes):
    places, row = [], 0
    for rows, _ in shapes:
        places.append(row)
        row += rows if rows == 1 else -(-rows // 8) * 8
    return places, -(-(row + 1) // 16) * 16


def backward_kernel(count, norm_scale, *refs):
    parts = refs[:count]
    summed, z_low, noise, ids = refs[count : count + 4]
    enc = [r[...] for r in refs[count + 4 : count + 11]]
    dec = [r[...] for r in refs[count + 11 : count + 16]]
    dp_out, pack_out = refs[count + 16 :]
    dg2 = parts[0][...]
    for part in parts[1:]:
        dg2 = dg2 + part[...]
    onehot = onehot_of(ids[...], dec[1].shape[0])
    unused, pull = jax.vjp(lambda z, *w: decoder_small(z, onehot, *w), z_low[...].astype(jnp.float32), *dec)
    dz, *dec_grads = pull(dg2)
    noise_rows = noise[...]
    unused, pull = jax.vjp(lambda s, *w: encoder_small(s, *w, noise_rows), summed[...], *enc)
    dz_low = dz.astype(jnp.bfloat16).astype(jnp.float32)
    dp, *enc_grads = pull((dz_low, jnp.full((1, 1), norm_scale, jnp.float32)))
    dp_out[...] = dp.astype(jnp.bfloat16)
    pack_out[...] = jnp.zeros_like(pack_out)
    grads = ordered(enc_grads + dec_grads)
    for row, grad in zip(pack_places([g.shape for g in grads])[0], grads):
        pack_out[row : row + grad.shape[0], : grad.shape[1]] = grad


def ordered(values):
    return [v for v in values if v.shape[0] > 1] + [v for v in values if v.shape[0] == 1]


STRIP = 16
TOP = 32767.0


def coded_rows(share, chunk):
    return chunk // 256 * share + STRIP


def code(values, out_ref, base, tile, share, strip):
    largest = jnp.maximum(jnp.max(jnp.abs(values), axis=0, keepdims=True), 1e-30)
    level = jnp.ceil(jnp.log2(largest) * 64.0 + 0.01)
    scaled = values * (TOP * jnp.exp2(level * (-1.0 / 64.0)))
    at = base + tile * share
    out_ref[at : at + share, :] = jnp.floor(scaled + 0.5).astype(jnp.int32).astype(jnp.int16)
    row = lax.broadcasted_iota(jnp.int32, (STRIP, 256), 0)
    return jnp.where(row == tile, level, strip)


def code_all(parts, out_ref, base, share):
    strip = jnp.zeros((STRIP, 256), jnp.float32)
    for tile, values in enumerate(parts):
        strip = code(values, out_ref, base, tile, share, strip)
    at = base + len(parts) * share
    out_ref[at : at + STRIP, :] = strip.astype(jnp.int32).astype(jnp.int16)


def decode(in_ref, base, tiles, share, tile):
    at = base + tiles * share
    level = in_ref[at : at + STRIP, :].astype(jnp.int32).astype(jnp.float32)[tile : tile + 1, :]
    at = base + tile * share
    values = in_ref[at : at + share, :].astype(jnp.int32).astype(jnp.float32)
    return values * (jnp.exp2(level * (1.0 / 64.0)) * (1.0 / TOP))


def give_shares(z, dw_ref, sent_ref, own_ref, other_ref):
    share, chunk = own_ref.shape

    def rows(which):
        return pl.ds(pl.multiple_of(which * share, 16), share)

    for place, which in enumerate((z ^ 1, z ^ 3)):
        parts = [dw_ref[rows(which), c : c + 256] for c in range(0, chunk, 256)]
        code_all(parts, sent_ref, place * coded_rows(share, chunk), share)
    own_ref[...] = dw_ref[rows(z), :]
    other_ref[...] = dw_ref[rows(z ^ 2), :]


def share_outputs(width, chunk, count, coded):
    if not coded:
        return [pl.BlockSpec((width, chunk), lambda j, h: (0, j))], [jax.ShapeDtypeStruct((width, count * chunk), jnp.float32)]
    share = width // 4
    rows = 2 * coded_rows(share, chunk)
    specs = [pl.BlockSpec((rows, 256), lambda j, h: (j, 0))] + [pl.BlockSpec((share, chunk), lambda j, h: (0, j))] * 2
    shapes = [jax.ShapeDtypeStruct((count * rows, 256), jnp.int16)]
    return specs, shapes + [jax.ShapeDtypeStruct((share, count * chunk), jnp.float32)] * 2


def join_kernel(got_ref, own_ref, other_ref, sent_ref, sum_ref, *, chunk):
    share, width = own_ref.shape
    tiles, rows = chunk // 256, coded_rows(share, chunk)
    for j in range(width // chunk):
        parts = []
        for tile in range(tiles):
            cols = slice(j * chunk + tile * 256, j * chunk + tile * 256 + 256)
            sum_ref[:, cols] = own_ref[:, cols] + decode(got_ref, 2 * j * rows, tiles, share, tile)
            parts.append(other_ref[:, cols] + decode(got_ref, (2 * j + 1) * rows, tiles, share, tile))
        code_all(parts, sent_ref, j * rows, share)


def total_kernel(sum_ref, got_ref, out_ref, *, chunk):
    share, width = sum_ref.shape
    tiles, rows = chunk // 256, coded_rows(share, chunk)
    for j in range(width // chunk):
        for tile in range(tiles):
            cols = slice(j * chunk + tile * 256, j * chunk + tile * 256 + 256)
            out_ref[:, cols] = sum_ref[:, cols] + decode(got_ref, j * rows, tiles, share, tile)


def line_call(kernel, args, out_shape, name):
    vmem = pl.BlockSpec(memory_space=pltpu.VMEM)
    return pl.pallas_call(
        kernel,
        in_specs=[vmem] * len(args),
        out_specs=[vmem] * len(out_shape),
        out_shape=out_shape,
        compiler_params=params_of(48),
        name=name,
    )(*args)


def line_start(pieces):
    if len(pieces) == 1:
        return [lax.psum_scatter(pieces[0], "dp", scatter_dimension=0, tiled=True)]
    return [lax.ppermute(pieces[0], "dp", [(i, i ^ 1) for i in range(4)]), *pieces[1:]]


def line_joined(state, chunk):
    if len(state) == 1:
        return state
    got, own, other = state
    sent = jax.ShapeDtypeStruct((got.shape[0] // 2, 256), jnp.int16)
    kernel = functools.partial(join_kernel, chunk=chunk)
    return line_call(kernel, state, [sent, jax.ShapeDtypeStruct(own.shape, jnp.float32)], "join")


def line_last(state):
    if len(state) == 1:
        return state
    return [lax.ppermute(state[0], "dp", [(i, i ^ 2) for i in range(4)]), state[1]]


def line_end(state, chunk):
    if len(state) == 1:
        return state[0]
    got, own = state
    kernel = functools.partial(total_kernel, chunk=chunk)
    return line_call(kernel, [own, got], [jax.ShapeDtypeStruct(own.shape, jnp.float32)], "total")[0]


def after(value, *others):
    return lax.optimization_barrier((value, *others))[0]


def chosen(core, encoder, kept_ref, got_ref):
    own = core == (0 if encoder else 1)
    return jnp.where(own, kept_ref[...], got_ref[...])


def project_kernel(started, half_ref, x_ref, kept_ref, got_ref, *refs):
    out_ref = refs[-1]
    size = x_ref.shape[0]
    rows = pl.ds(pl.multiple_of(pl.program_id(1) * size, 16), size)
    part = jnp.dot(x_ref[...], chosen(half_ref[1], True, kept_ref, got_ref), preferred_element_type=jnp.float32)

    @pl.when(pl.program_id(0) == 0)
    def first():
        out_ref[rows, :] = part + refs[0][rows, :] if started else part

    @pl.when(pl.program_id(0) != 0)
    def later():
        out_ref[rows, :] += part


def project(half, peaks, kept, got, before, first, got_first, count, chunk, per_half):
    cells, width = peaks.shape[0], kept.shape[1]
    started = before is not None
    whole = pl.BlockSpec((cells, width), lambda j, i, h: (0, 0))
    return pl.pallas_call(
        functools.partial(project_kernel, started),
        grid_spec=pltpu.PrefetchScalarGridSpec(
            num_scalar_prefetch=1,
            grid=(count, 2),
            in_specs=[
                pl.BlockSpec((cells // 2, chunk), lambda j, i, h: (i, h[0] * per_half + first + j)),
                pl.BlockSpec((chunk, width), lambda j, i, h: (h[0] * per_half + first + j, 0)),
                pl.BlockSpec((chunk, width), lambda j, i, h: (got_first + j, 0)),
            ]
            + [whole] * started,
            out_specs=whole,
        ),
        out_shape=jax.ShapeDtypeStruct((cells, width), jnp.float32),
        compiler_params=params_of(48),
        cost_estimate=pl.CostEstimate(
            flops=2 * cells * count * chunk * width, bytes_accessed=2 * cells * count * chunk, transcendentals=0
        ),
        name="project",
    )(half, peaks, kept, got, *([before] if started else []))


def regions_kernel(
    tile, rows_at_once, piece, started, coded, half_ref, x_ref, kept_ref, got_ref, g_ref, gt_ref, a_ref, fa_ref, ck_ref, cf_ref,
    *refs,
):
    outs = refs[1 if started else 0 :]
    dg_ref, st_ref = outs[:2]
    m0, m1, e0, e1, w_ref, dw_ref = outs[-6:] if coded else (*outs[3:], outs[2])
    cells, chunk = x_ref.shape
    blocks = cells // rows_at_once
    M, E = (m0, m1), (e0, e1)

    w_ref[...] = chosen(half_ref[1], False, kept_ref, got_ref)

    @pl.when(pl.program_id(0) == 0)
    def first():
        dg_ref[...] = refs[0][...] if started else jnp.zeros_like(dg_ref)

    def one_tile(t, carry):
        cols = pl.ds(pl.multiple_of(t * tile, 128), tile)
        w = w_ref[cols, :]
        w2 = jnp.concatenate([w, w], axis=1)
        wide = (8, tile)
        a = jnp.broadcast_to(a_ref[:, cols], wide)[None]
        fa = jnp.broadcast_to(fa_ref[:, cols], wide)[None]
        ck = jnp.broadcast_to(ck_ref[:, cols], wide)[None]

        def rows(i, o=0, n=rows_at_once):
            return pl.ds(pl.multiple_of(i * rows_at_once + o, 16), n)

        def logit(i, s, o, n):
            M[s][o : o + n, :] = lax.dot_general(
                g_ref[rows(i, o, n), :], w2, (((1,), (1,)), ((), ())), preferred_element_type=jnp.float32
            )

        def elementwise(i, s, o, sums):
            e_sum, l_sum = sums
            shape = (piece // 8, 8, tile)
            u = jnp.exp2(M[s][o : o + piece, :]).reshape(shape)
            cf = cf_ref[rows(i, o, piece), :]
            cf = jnp.concatenate([cf] * (tile // 128), axis=1).reshape(shape)
            seen = (x_ref[rows(i, o, piece), cols] * jnp.bfloat16(BIG)).astype(jnp.float32).reshape(shape)
            total = u + a
            rest = (total - fa * cf) + seen
            d = pltpu.reciprocal(rest, approx=True)
            slope = (u * ck) * (d - pltpu.reciprocal(total, approx=True))
            ratio = (d * total).reshape(piece // 16, 2, 8, tile)
            E[s][o : o + piece, :] = slope.reshape(piece, tile).astype(jnp.bfloat16)
            e_sum = e_sum + jnp.sum(slope, axis=0)
            l_sum = l_sum + jnp.sum(jnp.log2(ratio[:, 0] * ratio[:, 1]), axis=0)
            return e_sum, l_sum

        def cell_grad(i, s):
            dg_ref[rows(i), :] += jnp.dot(E[s][...], w, preferred_element_type=jnp.float32)

        def region_grad(i, s, start=False):
            part = jnp.dot(gt_ref[i], E[s][...], preferred_element_type=jnp.float32)
            if start:
                dw_ref[:, cols] = part
            else:
                dw_ref[:, cols] += part

        def step(i, s, sums, logits=True, grads=True, start=False):
            dots = rows_at_once // 2
            for o in range(0, rows_at_once, piece):
                if logits and o % dots == 0:
                    logit(i + 1, 1 - s, o, dots)
                sums = elementwise(i, s, o, sums)
                if grads and o == dots:
                    cell_grad(i - 1, 1 - s)
            if grads:
                region_grad(i - 1, 1 - s, start)
            return sums

        zero = jnp.zeros(wide, jnp.float32)
        sums = (zero, zero)
        logit(0, 0, 0, rows_at_once)
        sums = step(0, 0, sums, grads=False)
        for i in range(1, blocks):
            sums = step(i, i % 2, sums, logits=i < blocks - 1, start=i == 1)
        cell_grad(blocks - 1, (blocks - 1) % 2)
        region_grad(blocks - 1, (blocks - 1) % 2, blocks == 1)
        st_ref[0:8, cols] = sums[0]
        st_ref[8:16, cols] = sums[1]
        return carry

    lax.fori_loop(0, chunk // tile, one_tile, 0)
    if coded:
        give_shares(half_ref[2], dw_ref, *outs[2:5])


def regions_pass(half, peaks, kept, got, hidden, hidden_t, a, fa, ck, cf, before, first, at, count, chunk, per_half, coded):
    cells, width = peaks.shape[0], kept.shape[1]
    blocks, _, rows = hidden_t.shape
    tile, piece = min(256, chunk), 64
    started = before is not None
    whole = pl.BlockSpec((cells, width), lambda j, h: (0, 0))
    row = pl.BlockSpec((1, chunk), lambda j, h: (0, first + j))
    share_specs, share_shapes = share_outputs(width, chunk, count, coded)
    return pl.pallas_call(
        functools.partial(regions_kernel, tile, rows, piece, started, coded),
        grid_spec=pltpu.PrefetchScalarGridSpec(
            num_scalar_prefetch=1,
            grid=(count,),
            in_specs=[
                pl.BlockSpec((cells, chunk), lambda j, h: (0, h[0] * per_half + first + j)),
                pl.BlockSpec((chunk, width), lambda j, h: (h[0] * per_half + first + j, 0)),
                pl.BlockSpec((chunk, width), lambda j, h: (at + j, 0)),
                pl.BlockSpec((cells, 2 * width), lambda j, h: (0, 0)),
                pl.BlockSpec((blocks, width, rows), lambda j, h: (0, 0, 0)),
                row, row, row, whole,
            ]
            + [whole] * started,
            out_specs=[whole, pl.BlockSpec((16, chunk), lambda j, h: (0, j)), *share_specs],
            scratch_shapes=[pltpu.VMEM((rows, tile), jnp.float32)] * 2
            + [pltpu.VMEM((rows, tile), jnp.bfloat16)] * 2
            + [pltpu.VMEM((chunk, width), jnp.bfloat16)]
            + [pltpu.VMEM((width, chunk), jnp.float32)] * coded,
        ),
        out_shape=[
            jax.ShapeDtypeStruct((cells, width), jnp.float32),
            jax.ShapeDtypeStruct((16, count * chunk), jnp.float32),
            *share_shapes,
        ],
        compiler_params=params_of(56),
        cost_estimate=pl.CostEstimate(
            flops=10 * cells * count * chunk * width,
            bytes_accessed=2 * cells * count * chunk,
            transcendentals=16 * cells * count * chunk,
        ),
        name="regions",
    )(half, peaks, kept, got, hidden, hidden_t, a, fa, ck, cf, *([before] if started else []))


def outer_kernel(coded, half_ref, x_ref, left_ref, extra_ref, *outs):
    dw_ref = outs[-1] if coded else outs[0]
    width = dw_ref.shape[0]
    tile = min(256, x_ref.shape[1])
    for c in range(0, x_ref.shape[1], tile):
        cols = slice(c, c + tile)
        part = jnp.dot(left_ref[...], x_ref[:, cols], preferred_element_type=jnp.float32)
        dw_ref[:, cols] = part[:width]
        extra_ref[:, cols] = part[width:]
    if coded:
        give_shares(half_ref[2], dw_ref, *outs[:3])


def outer(half, peaks, left, first, count, chunk, per_half, coded):
    cells = peaks.shape[0]
    width = left.shape[0] - EXTRA
    share_specs, share_shapes = share_outputs(width, chunk, count, coded)
    return pl.pallas_call(
        functools.partial(outer_kernel, coded),
        grid_spec=pltpu.PrefetchScalarGridSpec(
            num_scalar_prefetch=1,
            grid=(count,),
            in_specs=[
                pl.BlockSpec((cells, chunk), lambda j, h: (0, h[0] * per_half + first + j)),
                pl.BlockSpec((width + EXTRA, cells), lambda j, h: (0, 0)),
            ],
            out_specs=[pl.BlockSpec((EXTRA, chunk), lambda j, h: (0, j)), *share_specs],
            scratch_shapes=[pltpu.VMEM((width, chunk), jnp.float32)] * coded,
        ),
        out_shape=[jax.ShapeDtypeStruct((EXTRA, count * chunk), jnp.float32), *share_shapes],
        compiler_params=params_of(48),
        cost_estimate=pl.CostEstimate(
            flops=2 * cells * count * chunk * width, bytes_accessed=2 * cells * count * chunk, transcendentals=0
        ),
        name="outer",
    )(half, peaks, left)


def part_of(values, which, size, axis=0):
    return lax.dynamic_slice_in_dim(values, which * size, size, axis)


def across_cores(values):
    return lax.ppermute(values, "pipe", [(0, 1), (1, 0)])


def shift_of(step, index, count):
    if count & (count - 1) == 0:
        return index ^ step
    return (index + step) % count


def scatter_cells(partial):
    cells = partial.shape[0]
    pipe, mine, count = lax.axis_index("pipe"), lax.axis_index("tensor"), lax.axis_size("tensor")
    half = cells // 2
    got = across_cores(part_of(partial, 1 - pipe, half))
    chip_sum = part_of(partial, pipe, half) + got
    rows = half // count
    pieces = [part_of(chip_sum, mine, rows)]
    for step in range(1, count):
        there = shift_of(step, mine, count)
        route = [(i, shift_of(step, i, count)) for i in range(count)]
        pieces.append(lax.ppermute(part_of(chip_sum, there, rows), "tensor", route))
    return pieces


def gather_cells(own):
    count = lax.axis_size("tensor")
    pieces = [own]
    for step in range(1, count):
        route = [(i, shift_of(step, i, count)) for i in range(count)]
        pieces.append(lax.ppermute(own, "tensor", route))
    return pieces + [across_cores(piece) for piece in pieces]


def rows_at(place_ref, index, count, rows):
    core, mine = place_ref[0], place_ref[1]
    step = index % count
    if count & (count - 1) == 0:
        sender = mine ^ step
    else:
        sender = lax.rem(mine - step + count, jnp.int32(count))
    here = core if index < count else 1 - core
    return (here * count + sender) * rows


def hidden_kernel(count, place_ref, *refs):
    pieces, (wide_ref, turned_ref, all_s) = refs[:-3], refs[-3:]
    rows, width = pieces[0].shape
    for index, piece in enumerate(pieces):
        at = pl.ds(pl.multiple_of(rows_at(place_ref, index, count, rows), 16), rows)
        all_s[at, :] = piece[...].astype(jnp.float32)
    scaled = all_s[...] * (-LOG2E)
    high = scaled.astype(jnp.bfloat16)
    wide_ref[:, :width] = high
    wide_ref[:, width:] = (scaled - high.astype(jnp.float32)).astype(jnp.bfloat16)
    size = turned_ref.shape[2]
    for block in range(turned_ref.shape[0]):
        turned_ref[block] = jnp.transpose(all_s[block * size : (block + 1) * size, :]).astype(jnp.bfloat16)


def left_kernel(count, place_ref, log_ref, *refs):
    pieces, (left_ref, all_s) = refs[:-2], refs[-2:]
    rows, width = pieces[0].shape
    for index, piece in enumerate(pieces):
        at = pl.ds(pl.multiple_of(rows_at(place_ref, index, count, rows), 16), rows)
        all_s[at, :] = piece[...].astype(jnp.float32)
    left_ref[:width, :] = jnp.transpose(all_s[...]).astype(jnp.bfloat16)
    left_ref[width:, :] = log_ref[...]


def assemble(kernel, place, pieces, before, out_shape, name):
    vmem = pl.BlockSpec(memory_space=pltpu.VMEM)
    rows, width = pieces[0].shape
    return pl.pallas_call(
        functools.partial(kernel, len(pieces) // 2),
        in_specs=[pl.BlockSpec(memory_space=pltpu.SMEM)] + [vmem] * (len(before) + len(pieces)),
        out_specs=[vmem] * len(out_shape),
        out_shape=out_shape,
        scratch_shapes=[pltpu.VMEM((rows * len(pieces), width), jnp.float32)],
        compiler_params=params_of(32),
        name=name,
    )(place, *before, *pieces)


def exchange_bits(axis):
    count = lax.axis_size(axis)
    return [1 << i for i in range((count - 1).bit_length())]


def exchanged(values, axis, bit):
    count = lax.axis_size(axis)
    return values + lax.ppermute(values, axis, [(i, i ^ bit) for i in range(count)])


def all_sum(values, axes):
    for axis in axes:
        for bit in exchange_bits(axis):
            values = exchanged(values, axis, bit)
    return values


def join_cores(own):
    other = across_cores(own)
    first = lax.axis_index("pipe") == 0
    return jnp.where(first, own, other), jnp.where(first, other, own)


def three_terms(values):
    high = values.astype(jnp.bfloat16)
    rest = values - high.astype(jnp.float32)
    middle = rest.astype(jnp.bfloat16)
    return high, middle, (rest - middle.astype(jnp.float32)).astype(jnp.bfloat16)


def body(
    peak_data,
    region_weights,
    out_bias,
    region_factor,
    region_keep,
    cell_factor,
    batch_ids,
    latent_noise,
    enc_bias_in,
    enc_square,
    enc_bias_two,
    enc_heads,
    head_bias,
    dec_first,
    dec_bias_one,
    dec_square,
    dec_bias_two,
):
    cells, regions_local = peak_data.shape
    weight = region_weights[0]
    width = weight.shape[1]
    latent = latent_noise.shape[1]
    batches = dec_first.shape[0] - latent
    window = -(-regions_local // 256) * 128
    overlap = 2 * window - regions_local
    pipe, mine, tensors = lax.axis_index("pipe"), lax.axis_index("tensor"), lax.axis_size("tensor")
    cell_total = cells * lax.axis_size("dp")
    region_total = regions_local * tensors
    norm_scale = float(cell_total) ** (-0.5)

    def of_core(values, core, axis=0):
        return lax.dynamic_slice_in_dim(values, core * (regions_local - window), window, axis)

    keep = of_core(region_keep, pipe).astype(jnp.float32)
    dp_at = lax.axis_index("dp")
    place = jnp.stack([pipe, mine, dp_at]).astype(jnp.int32)
    chunk = next(c for c in (1792, 256, 128) if window % c == 0 and (regions_local - window) % c == 0)
    chunks = window // chunk
    ahead = min(2, chunks - 1) * chunk
    coded = lax.axis_size("dp") == 4 and chunk % 256 == 0
    if overlap:
        mine_alone = (pipe == 0) | (jnp.arange(window) >= overlap)
        keep = jnp.where(mine_alone, keep, 0.0)
        peak_data = of_core(peak_data, pipe, 1)
        own = of_core(weight, pipe)
        got = across_cores(of_core(weight, 1 - pipe))
        kept_enc = got_enc = jnp.where(mine_alone[:, None], jnp.where(pipe == 0, own, got), 0)
        weight = jnp.where(pipe == 0, got, own)
        got_spans = [(weight, 0, 0, chunks)]
        got_parts = [(kept_enc, got_enc, 0, 0, chunks)]
        half = jnp.stack([jnp.zeros_like(place[0]), place[0], place[2]])
    else:
        other_at = (1 - pipe) * (regions_local - window)
        got_first = across_cores(lax.dynamic_slice_in_dim(weight, other_at, ahead, 0))
        got_rest = across_cores(lax.dynamic_slice_in_dim(weight, other_at + ahead, window - ahead, 0))
        got_parts = [(weight, got_first, 0, 0, ahead // chunk), (weight, got_rest, ahead // chunk, 0, chunks - ahead // chunk)]
        cut = ahead // chunk
        middle = cut + (chunks - cut + 1) // 2
        got_spans = [(got_first, 0, 0, cut), (got_rest, 0, cut, middle), (got_rest, middle - cut, middle, chunks)]
        half = jnp.stack([place[0], place[0], place[2]])

    own_rows = cells // (2 * tensors)
    own_at = pipe * tensors + mine
    noise_own = part_of(latent_noise, own_at, own_rows)
    ids_own = part_of(batch_ids[:, None], own_at, own_rows)
    heads_t = jnp.transpose(enc_heads)
    enc = (
        enc_bias_in[None], enc_square, enc_bias_two[None], heads_t[:latent], heads_t[latent:],
        head_bias[None, :latent], head_bias[None, latent:],
    )
    dec = (dec_first[:latent], dec_first[latent:], dec_bias_one[None], dec_square, dec_bias_two[None])

    a = jnp.exp(of_core(out_bias, pipe))[None]
    fa = a * of_core(region_factor, pipe)[None]
    ck = (keep * norm_scale)[None]
    cf_wide = jnp.broadcast_to(cell_factor[:, None], (cells, 128))
    logs = jnp.concatenate(
        [jnp.ones((1, cells), jnp.bfloat16)]
        + [t[None] for t in three_terms(jnp.log(cell_factor))]
        + [jnp.zeros((EXTRA - 4, cells), jnp.bfloat16)],
        axis=0,
    )
    early = (noise_own, ids_own, enc, dec, a, fa, ck, cf_wide, logs)
    kept_first, got_first, *span = got_parts[0]
    got_first, early = lax.optimization_barrier((got_first, early))
    noise_own, ids_own, enc, dec, a, fa, ck, cf_wide, logs = early
    got_parts[0] = (kept_first, got_first, *span)

    vmem = pl.BlockSpec(memory_space=pltpu.VMEM)
    partial = None
    for kept_w, got_w, first, at, count in got_parts:
        partial = project(half, peak_data, kept_w, got_w, partial, first, at, count, chunk, chunks)
    pieces = scatter_cells(partial)
    summed, z_low, g2_own, kl_sum = pl.pallas_call(
        functools.partial(forward_kernel, len(pieces)),
        in_specs=[vmem] * (len(pieces) + 14),
        out_specs=[vmem] * 4,
        out_shape=[
            jax.ShapeDtypeStruct((own_rows, width), jnp.float32),
            jax.ShapeDtypeStruct((own_rows, latent), jnp.bfloat16),
            jax.ShapeDtypeStruct((own_rows, width), jnp.bfloat16),
            jax.ShapeDtypeStruct((1, 1), jnp.float32),
        ],
        compiler_params=params_of(32),
        name="small_forward",
    )(*pieces, noise_own, ids_own, *enc, *dec)
    rows_b = min(512, cells // 2)
    hidden, hidden_t = assemble(
        hidden_kernel, place, gather_cells(g2_own), [],
        [
            jax.ShapeDtypeStruct((cells, 2 * width), jnp.bfloat16),
            jax.ShapeDtypeStruct((cells // rows_b, width, rows_b), jnp.bfloat16),
        ],
        "hidden",
    )

    dg2, lines, stats = None, [], []
    for got_w, at, first, end in got_spans:
        if len(lines) > 1:
            lines[-2] = line_joined(lines[-2], chunk)
            dg2 = after(dg2, *lines[-2])
            lines[-2] = line_last(lines[-2])
        dg2, st, *shares = regions_pass(
            half, peak_data, weight, got_w, hidden, hidden_t, a, fa, ck, cf_wide, dg2, first, at, end - first, chunk,
            chunks, coded,
        )
        lines.append(line_start(shares))
        stats.append(st)
    stats = jnp.concatenate(stats, axis=1)

    if len(lines) > 1:
        lines[-2] = line_last(line_joined(lines[-2], chunk))
    pieces = scatter_cells(dg2)
    grad_shapes = [w.shape for w in ordered(enc + dec)]
    places, pack_rows = pack_places(grad_shapes)
    dp_own, pack = pl.pallas_call(
        functools.partial(backward_kernel, len(pieces), norm_scale),
        in_specs=[vmem] * (len(pieces) + 16),
        out_specs=[vmem] * 2,
        out_shape=[
            jax.ShapeDtypeStruct((own_rows, width), jnp.bfloat16),
            jax.ShapeDtypeStruct((pack_rows, width), jnp.float32),
        ],
        compiler_params=params_of(32),
        name="small_backward",
    )(*pieces, summed, z_low, noise_own, ids_own, *enc, *dec)
    (left,) = assemble(
        left_kernel, place, gather_cells(dp_own), [logs],
        [jax.ShapeDtypeStruct((width + EXTRA, cells), jnp.bfloat16)],
        "left",
    )
    cuts = [0, 2, 5, chunks] if chunks == 7 else [0, chunks]
    extras, enc_lines = [], []
    under_way = [(lines, lines.pop())]
    for first, end in zip(cuts[:-1], cuts[1:]):
        if first:
            where, line = under_way.pop(0)
            line = line_joined(line, chunk)
            left = after(left, line[0])
            where.append(line_last(line))
        extra, *shares = outer(half, peak_data, left, first, end - first, chunk, chunks, coded)
        under_way.append((enc_lines, line_start(shares)))
        extras.append(extra)
    extra = jnp.concatenate(extras, axis=1)
    newest = under_way[-1][1][0]
    joined = []
    for where, line in under_way:
        line = line_joined(line, chunk)
        joined.append(line[0])
        where.append(line_last(line))

    dec_own = [line_end(line, chunk) for line in lines]
    dec_got = [lax.ppermute(share, "pipe", [(0, 1)]) for share in dec_own]
    enc_own = [line_end(line, chunk) for line in enc_lines]
    enc_got = [lax.ppermute(share, "pipe", [(1, 0)]) for share in enc_own]
    is_first = pipe == 0
    lower = jnp.where(is_first, jnp.concatenate(enc_own, axis=1), jnp.concatenate(dec_got, axis=1))
    upper = jnp.where(is_first, jnp.concatenate(enc_got, axis=1), jnp.concatenate(dec_own, axis=1))
    region_grad = jnp.transpose(jnp.concatenate([lower, upper[:, overlap:]], axis=1))[None]

    seen, seen_log = extra[0], extra[1] + extra[2] + extra[3]
    per_region = LN2 * jnp.sum(stats[8:], axis=0) + seen * (BIG_BITS * LN2 - jnp.log(fa[0])) - seen_log
    loss = jnp.sum(keep * per_region) + kl_sum[0, 0]
    pack = pack.at[pack_rows - 1, 0].set(loss)
    pack_half = pack_rows // 2
    pack = part_of(pack, pipe, pack_half) + across_cores(part_of(pack, 1 - pipe, pack_half))
    pack = all_sum(after(pack, newest, joined[0]), ["tensor"])
    sums = jnp.concatenate([pack, jnp.sum(stats[:8], axis=0).reshape(-1, 128)], axis=0)
    sums = after(sums, joined[-1])
    for bit in exchange_bits("dp"):
        if bit > 1:
            sums = after(sums, enc_lines[-1][0])
        sums = exchanged(sums, "dp", bit)
    lower, upper = join_cores(sums)
    pack = jnp.concatenate([lower[:pack_half], upper[:pack_half]], axis=0)
    bias_grad = jnp.concatenate([lower[pack_half:].reshape(-1), upper[pack_half:].reshape(-1)[overlap:]])
    small = {}
    shapes = list(enumerate(w.shape for w in enc + dec))
    named = [s for s in shapes if s[1][0] > 1] + [s for s in shapes if s[1][0] == 1]
    for row, (index, shape) in zip(places, named):
        small[index] = pack[row : row + shape[0], : shape[1]]
    (d_bias_in, d_square, d_bias_two, d_mean_w, d_var_w, d_mean_b, d_var_b, d_first_z, d_first_b, d_bias_one, d_dec_square,
     d_dec_bias_two) = [small[i] for i in range(len(small))]
    mean_loss = pack[pack_rows - 1, 0] / (cell_total * region_total)
    return (
        region_grad,
        bias_grad,
        d_bias_in[0],
        d_square,
        d_bias_two[0],
        jnp.transpose(jnp.concatenate([d_mean_w, d_var_w], axis=0)),
        jnp.concatenate([d_mean_b[0], d_var_b[0]], axis=0),
        jnp.concatenate([d_first_z, d_first_b], axis=0),
        d_bias_one[0],
        d_dec_square,
        d_dec_bias_two[0],
        mean_loss,
    )


def solution(mesh):
    in_specs = (
        P("dp", "tensor"),
        P("pipe", "tensor", None),
        P("tensor"),
        P("tensor"),
        P("tensor"),
        P("dp"),
        P("dp"),
        P("dp", None),
        *[P()] * 9,
    )
    out_specs = (P("pipe", "tensor", "dp"), P("tensor"), *[P()] * 10)
    return jax.shard_map(body, mesh=mesh, in_specs=in_specs, out_specs=out_specs, check_vma=False)
```

```python
import functools

import jax
import jax.numpy as jnp
import numpy as np
from jax import lax
from jax.experimental import pallas as pl
from jax.experimental.pallas import tpu as pltpu
from jax.sharding import PartitionSpec as P

EXACT = lax.Precision.HIGHEST
NORM_EPS = 1e-05
LOG2E = float(np.log2(np.e))
LN2 = float(np.log(2.0))
BIG_BITS = 56
BIG = float(2.0**BIG_BITS)
MIB = 1 << 20


def params_of(mib):
    return pltpu.CompilerParams(vmem_limit_bytes=mib * MIB)


def layer_norm(values):
    centred = values - jnp.mean(values, axis=-1, keepdims=True)
    return centred * lax.rsqrt(jnp.mean(centred * centred, axis=-1, keepdims=True) + NORM_EPS)


def silu(values):
    return values * jax.nn.sigmoid(values)


def mm(a, b):
    return lax.dot_general(a, b, (((1,), (0,)), ((), ())), precision=EXACT, preferred_element_type=jnp.float32)


def mm_t(a, b):
    return lax.dot_general(a, b, (((1,), (1,)), ((), ())), precision=EXACT, preferred_element_type=jnp.float32)


def encoder_small(summed, bias_in, square, bias_two, mean_w, var_w, mean_b, var_b, noise_rows):
    hidden = silu(layer_norm(summed + bias_in))
    hidden = silu(layer_norm(mm(hidden, square) + bias_two))
    average = mm_t(hidden, mean_w) + mean_b
    variance = jnp.exp(mm_t(hidden, var_w) + var_b) + 0.0001
    sample = average + jnp.sqrt(variance) * noise_rows
    kl_rows = 0.5 * jnp.sum(average * average + variance - jnp.log(variance) - 1.0, axis=1, keepdims=True)
    return (sample, jnp.sum(kl_rows, axis=0, keepdims=True))


def decoder_small(latent_rows, onehot, first_z, first_b, bias_one, square, bias_two):
    hidden = silu(layer_norm(mm(latent_rows, first_z) + mm(onehot, first_b) + bias_one))
    return silu(layer_norm(mm(hidden, square) + bias_two))


def onehot_of(ids, width):
    codes = lax.broadcasted_iota(jnp.int32, (ids.shape[0], width), 1)
    return (ids == codes).astype(jnp.float32)


def forward_kernel(count, *refs):
    parts = refs[:count]
    noise, ids = refs[count : count + 2]
    enc = [r[...] for r in refs[count + 2 : count + 9]]
    dec = [r[...] for r in refs[count + 9 : count + 14]]
    summed_out, z_out, g2_out, kl_out = refs[count + 14 :]
    summed = parts[0][...]
    for part in parts[1:]:
        summed = summed + part[...]
    sample, kl_sum = encoder_small(summed, *enc, noise[...])
    z_low = sample.astype(jnp.bfloat16)
    hidden = decoder_small(z_low.astype(jnp.float32), onehot_of(ids[...], dec[1].shape[0]), *dec)
    summed_out[...] = summed
    z_out[...] = z_low
    g2_out[...] = hidden.astype(jnp.bfloat16)
    kl_out[...] = kl_sum


def pack_places(shapes):
    places, row = [], 0
    for rows, _ in shapes:
        places.append(row)
        row += rows if rows == 1 else -(-rows // 8) * 8
    return places, -(-(row + 1) // 16) * 16


def backward_kernel(count, norm_scale, calls, *refs):
    parts = refs[:count]
    summed, z_low, noise, ids = refs[count : count + 4]
    enc = [r[...] for r in refs[count + 4 : count + 11]]
    dec = [r[...] for r in refs[count + 11 : count + 16]]
    owed = refs[count + 16]
    losses = refs[count + 17 : count + 17 + calls]
    dp_out, pack_out = refs[count + 17 + calls :]
    dg2 = parts[0][...]
    for part in parts[1:]:
        dg2 = dg2 + part[...]
    onehot = onehot_of(ids[...], dec[1].shape[0])
    unused, pull = jax.vjp(lambda z, *w: decoder_small(z, onehot, *w), z_low[...].astype(jnp.float32), *dec)
    dz, *dec_grads = pull(dg2)
    noise_rows = noise[...]
    unused, pull = jax.vjp(lambda s, *w: encoder_small(s, *w, noise_rows), summed[...], *enc)
    dz_low = dz.astype(jnp.bfloat16).astype(jnp.float32)
    dp, *enc_grads = pull((dz_low, jnp.full((1, 1), norm_scale, jnp.float32)))
    dp_out[...] = dp.astype(jnp.bfloat16)
    pack_out[...] = jnp.zeros_like(pack_out)
    grads = ordered(enc_grads + dec_grads)
    for row, grad in zip(pack_places([g.shape for g in grads])[0], grads):
        pack_out[row : row + grad.shape[0], : grad.shape[1]] = grad
    loss = losses[0][...]
    for ref in losses[1:]:
        loss = loss + ref[...]
    loss = jnp.sum(jnp.sum(loss, axis=0, keepdims=True), axis=1, keepdims=True) * (LN2 / norm_scale) + owed[...]
    pack_out[pack_out.shape[0] - 1 :, 0:1] = loss


def unpack_kernel(cuts, lower_ref, upper_ref, *refs):
    pack = refs[-1]
    half = lower_ref.shape[0]
    pack[:half, :] = lower_ref[...]
    pack[half:, :] = upper_ref[...]
    for cut, out in zip(cuts, refs[:-1]):
        at = 0
        for row, rows, columns in cut:
            out[at : at + rows, :] = pack[row : row + rows, :columns]
            at += rows


class RankedShape:
    def __init__(self, rows, columns, index):
        self.shape, self.index = (rows, columns), index


def ordered(values):
    return [v for v in values if v.shape[0] > 1] + [v for v in values if v.shape[0] == 1]


STRIP = 16
TOP = 32767.0


def coded_rows(share, chunk):
    return chunk // 256 * share + STRIP


def code(values, out_ref, base, tile, share, strip):
    largest = jnp.maximum(jnp.max(jnp.abs(values), axis=0, keepdims=True), 1e-30)
    level = jnp.ceil(jnp.log2(largest) * 64.0 + 0.01)
    scaled = values * (TOP * jnp.exp2(level * (-1.0 / 64.0)))
    at = base + tile * share
    out_ref[at : at + share, :] = jnp.floor(scaled + 0.5).astype(jnp.int32).astype(jnp.int16)
    row = lax.broadcasted_iota(jnp.int32, (STRIP, 256), 0)
    return jnp.where(row == tile, level, strip)


def code_all(parts, out_ref, base, share):
    strip = jnp.zeros((STRIP, 256), jnp.float32)
    for tile, values in enumerate(parts):
        strip = code(values, out_ref, base, tile, share, strip)
    at = base + len(parts) * share
    out_ref[at : at + STRIP, :] = strip.astype(jnp.int32).astype(jnp.int16)


def decode(in_ref, base, tiles, share, tile):
    at = base + tiles * share
    level = in_ref[at : at + STRIP, :].astype(jnp.int32).astype(jnp.float32)[tile : tile + 1, :]
    at = base + tile * share
    values = in_ref[at : at + share, :].astype(jnp.int32).astype(jnp.float32)
    return values * (jnp.exp2(level * (1.0 / 64.0)) * (1.0 / TOP))


def give_shares(z, dw_ref, sent_ref, own_ref, other_ref):
    share, chunk = own_ref.shape

    def rows(which):
        return pl.ds(pl.multiple_of(which * share, 16), share)

    for place, which in enumerate((z ^ 1, z ^ 3)):
        parts = [dw_ref[rows(which), c : c + 256] for c in range(0, chunk, 256)]
        code_all(parts, sent_ref, place * coded_rows(share, chunk), share)
    own_ref[...] = dw_ref[rows(z), :]
    other_ref[...] = dw_ref[rows(z ^ 2), :]


def share_outputs(width, chunk, count, coded):
    if not coded:
        return [pl.BlockSpec((width, chunk), lambda j, h: (0, j))], [jax.ShapeDtypeStruct((width, count * chunk), jnp.float32)]
    share = width // 4
    rows = 2 * coded_rows(share, chunk)
    specs = [pl.BlockSpec((rows, 256), lambda j, h: (j, 0))] + [pl.BlockSpec((share, chunk), lambda j, h: (0, j))] * 2
    shapes = [jax.ShapeDtypeStruct((count * rows, 256), jnp.int16)]
    return specs, shapes + [jax.ShapeDtypeStruct((share, count * chunk), jnp.float32)] * 2


def join_kernel(got_ref, own_ref, other_ref, sent_ref, sum_ref, *, chunk):
    share, width = own_ref.shape
    tiles, rows = chunk // 256, coded_rows(share, chunk)
    for j in range(width // chunk):
        parts = []
        for tile in range(tiles):
            cols = slice(j * chunk + tile * 256, j * chunk + tile * 256 + 256)
            sum_ref[:, cols] = own_ref[:, cols] + decode(got_ref, 2 * j * rows, tiles, share, tile)
            parts.append(other_ref[:, cols] + decode(got_ref, (2 * j + 1) * rows, tiles, share, tile))
        code_all(parts, sent_ref, j * rows, share)


def total_kernel(sum_ref, got_ref, out_ref, *, chunk):
    share, width = sum_ref.shape
    tiles, rows = chunk // 256, coded_rows(share, chunk)
    for j in range(width // chunk):
        for tile in range(tiles):
            cols = slice(j * chunk + tile * 256, j * chunk + tile * 256 + 256)
            out_ref[:, cols] = sum_ref[:, cols] + decode(got_ref, j * rows, tiles, share, tile)


def one_step(kernel, args, out_shape, name, place=None, scratch=()):
    def whole(array):
        return pl.BlockSpec(array.shape, lambda i, rank=len(array.shape): (0,) * rank)

    front = [] if place is None else [place]
    return pl.pallas_call(
        kernel,
        grid=(1,),
        in_specs=[pl.BlockSpec(memory_space=pltpu.SMEM)] * len(front) + [whole(x) for x in args],
        out_specs=[whole(x) for x in out_shape],
        out_shape=list(out_shape),
        scratch_shapes=list(scratch),
        compiler_params=params_of(48),
        name=name,
    )(*front, *args)


def line_start(pieces):
    if len(pieces) == 1:
        return [lax.psum_scatter(pieces[0], "dp", scatter_dimension=0, tiled=True)]
    return [lax.ppermute(pieces[0], "dp", [(i, i ^ 1) for i in range(4)]), *pieces[1:]]


def line_joined(state, chunk):
    if len(state) == 1:
        return state
    got, own, other = state
    sent = jax.ShapeDtypeStruct((got.shape[0] // 2, 256), jnp.int16)
    kernel = functools.partial(join_kernel, chunk=chunk)
    return one_step(kernel, state, [sent, jax.ShapeDtypeStruct(own.shape, jnp.float32)], "join")


def line_last(state):
    if len(state) == 1:
        return state
    return [lax.ppermute(state[0], "dp", [(i, i ^ 2) for i in range(4)]), state[1]]


def line_end(state, chunk):
    if len(state) == 1:
        return state[0]
    got, own = state
    kernel = functools.partial(total_kernel, chunk=chunk)
    return one_step(kernel, [own, got], [jax.ShapeDtypeStruct(own.shape, jnp.float32)], "total")[0]


def after(value, *others):
    return lax.optimization_barrier((value, *others))[0]


def chosen(core, encoder, kept_ref, got_ref):
    own = core == (0 if encoder else 1)
    return jnp.where(own, kept_ref[...], got_ref[...])


def weight_specs(chunk, width, per_half, first, got_first, encoder):
    owner = 0 if encoder else 1

    def kept(j, h):
        return (jnp.where(h[1] == owner, h[0] * per_half + first + j, 0), 0)

    def got(j, h):
        return (jnp.where(h[1] == owner, 0, got_first + j), 0)

    return [pl.BlockSpec((chunk, width), kept), pl.BlockSpec((chunk, width), got)]


def project_kernel(started, half_ref, x_ref, kept_ref, got_ref, keep_ref, log_ref, *refs):
    out_ref, seen_ref = refs[-2:]
    chunk, width = kept_ref.shape
    keep = keep_ref[...]
    row = lax.broadcasted_iota(jnp.int32, (width, chunk), 0)
    terms = jnp.where(row == 0, keep, 0.0)
    rest = keep * log_ref[...]
    for place in range(1, 4):
        high = rest.astype(jnp.bfloat16).astype(jnp.float32)
        terms = jnp.where(row == place, high, terms)
        rest = rest - high
    right = jnp.concatenate([chosen(half_ref[1], True, kept_ref, got_ref), jnp.transpose(terms).astype(jnp.bfloat16)], axis=1)
    part = jnp.dot(x_ref[...], right, preferred_element_type=jnp.float32)

    @pl.when(pl.program_id(0) == 0)
    def first():
        out_ref[...] = part[:, :width] + refs[0][...] if started else part[:, :width]
        seen_ref[...] = part[:, width:] + refs[1][...] if started else part[:, width:]

    @pl.when(pl.program_id(0) != 0)
    def later():
        out_ref[...] += part[:, :width]
        seen_ref[...] += part[:, width:]


def project(half, peaks, kept, got, keep, log_fa, before, first, got_first, count, chunk, per_half):
    cells, width = peaks.shape[0], kept.shape[1]
    whole = pl.BlockSpec((cells, width), lambda j, h: (0, 0))
    row = pl.BlockSpec((1, chunk), lambda j, h: (0, first + j))
    return pl.pallas_call(
        functools.partial(project_kernel, bool(before)),
        grid_spec=pltpu.PrefetchScalarGridSpec(
            num_scalar_prefetch=1,
            grid=(count,),
            in_specs=[
                pl.BlockSpec((cells, chunk), lambda j, h: (0, h[0] * per_half + first + j)),
                *weight_specs(chunk, width, per_half, first, got_first, True),
                row,
                row,
            ]
            + [whole] * len(before),
            out_specs=[whole, whole],
        ),
        out_shape=[jax.ShapeDtypeStruct((cells, width), jnp.float32)] * 2,
        compiler_params=params_of(48),
        cost_estimate=pl.CostEstimate(
            flops=2 * cells * count * chunk * width, bytes_accessed=2 * cells * count * chunk, transcendentals=0
        ),
        name="project",
    )(half, peaks, kept, got, keep, log_fa, *before)


def regions_kernel(
    tile, rows_at_once, piece, started, coded, half_ref, x_ref, kept_ref, got_ref, g_ref, gt_ref, a_ref, fa_ref, ck_ref, cf_ref,
    *refs,
):
    outs = refs[1 if started else 0 :]
    dg_ref, bias_ref, loss_ref = outs[:3]
    m0, m1, e0, e1, w_ref, dw_ref = outs[-6:] if coded else (*outs[4:], outs[3])
    cells, chunk = x_ref.shape
    blocks = cells // rows_at_once
    M, E = (m0, m1), (e0, e1)

    w_ref[...] = chosen(half_ref[1], False, kept_ref, got_ref)

    @pl.when(pl.program_id(0) == 0)
    def first():
        dg_ref[...] = refs[0][...] if started else jnp.zeros_like(dg_ref)
        loss_ref[...] = jnp.zeros_like(loss_ref)

    def one_tile(t, carry):
        cols = pl.ds(pl.multiple_of(t * tile, 128), tile)
        w = w_ref[cols, :]
        w2 = jnp.concatenate([w, w], axis=1)
        wide = (8, tile)
        a = jnp.broadcast_to(a_ref[:, cols], wide)[None]
        fa = jnp.broadcast_to(fa_ref[:, cols], wide)[None]
        ck = jnp.broadcast_to(ck_ref[:, cols], wide)[None]

        def rows(i, o=0, n=rows_at_once):
            return pl.ds(pl.multiple_of(i * rows_at_once + o, 16), n)

        def logit(i, s, o, n):
            M[s][o : o + n, :] = lax.dot_general(
                g_ref[rows(i, o, n), :], w2, (((1,), (1,)), ((), ())), preferred_element_type=jnp.float32
            )

        def elementwise(i, s, o, sums):
            e_sum, l_sum = sums
            shape = (piece // 8, 8, tile)
            u = jnp.exp2(M[s][o : o + piece, :]).reshape(shape)
            cf = cf_ref[rows(i, o, piece), :]
            cf = jnp.concatenate([cf] * (tile // 128), axis=1).reshape(shape)
            seen = (x_ref[rows(i, o, piece), cols] * jnp.bfloat16(BIG)).astype(jnp.float32).reshape(shape)
            total = u + a
            rest = (total - fa * cf) + seen
            d = pltpu.reciprocal(rest, approx=True)
            slope = (u * ck) * (d - pltpu.reciprocal(total, approx=True))
            ratio = (d * total).reshape(piece // 16, 2, 8, tile)
            E[s][o : o + piece, :] = slope.reshape(piece, tile).astype(jnp.bfloat16)
            e_sum = e_sum + jnp.sum(slope, axis=0)
            l_sum = l_sum + jnp.sum(jnp.log2(ratio[:, 0] * ratio[:, 1]), axis=0)
            return e_sum, l_sum

        def cell_grad(i, s):
            dg_ref[rows(i), :] += jnp.dot(E[s][...], w, preferred_element_type=jnp.float32)

        def region_grad(i, s, start=False):
            part = jnp.dot(gt_ref[i], E[s][...], preferred_element_type=jnp.float32)
            if start:
                dw_ref[:, cols] = part
            else:
                dw_ref[:, cols] += part

        def step(i, s, sums, logits=True, grads=True, start=False):
            dots = rows_at_once // 2
            for o in range(0, rows_at_once, piece):
                if logits and o % dots == 0:
                    logit(i + 1, 1 - s, o, dots)
                sums = elementwise(i, s, o, sums)
                if grads and o == dots:
                    cell_grad(i - 1, 1 - s)
            if grads:
                region_grad(i - 1, 1 - s, start)
            return sums

        zero = jnp.zeros(wide, jnp.float32)
        sums = (zero, zero)
        logit(0, 0, 0, rows_at_once)
        sums = step(0, 0, sums, grads=False)
        for i in range(1, blocks):
            sums = step(i, i % 2, sums, logits=i < blocks - 1, start=i == 1)
        cell_grad(blocks - 1, (blocks - 1) % 2)
        region_grad(blocks - 1, (blocks - 1) % 2, blocks == 1)
        bias_ref[:, cols] = jnp.sum(sums[0], axis=0, keepdims=True)
        kept = sums[1] * ck[0]
        for c in range(0, tile, 128):
            loss_ref[...] += kept[:, c : c + 128]
        return carry

    lax.fori_loop(0, chunk // tile, one_tile, 0)
    if coded:
        give_shares(half_ref[2], dw_ref, *outs[3:6])


def regions_pass(half, peaks, kept, got, hidden, hidden_t, a, fa, ck, cf, before, first, at, count, chunk, per_half, coded):
    cells, width = peaks.shape[0], kept.shape[1]
    blocks, _, rows = hidden_t.shape
    tile, piece = min(256, chunk), 64
    started = before is not None
    whole = pl.BlockSpec((cells, width), lambda j, h: (0, 0))
    row = pl.BlockSpec((1, chunk), lambda j, h: (0, first + j))
    share_specs, share_shapes = share_outputs(width, chunk, count, coded)
    return pl.pallas_call(
        functools.partial(regions_kernel, tile, rows, piece, started, coded),
        grid_spec=pltpu.PrefetchScalarGridSpec(
            num_scalar_prefetch=1,
            grid=(count,),
            in_specs=[
                pl.BlockSpec((cells, chunk), lambda j, h: (0, h[0] * per_half + first + j)),
                *weight_specs(chunk, width, per_half, first, at, False),
                pl.BlockSpec((cells, 2 * width), lambda j, h: (0, 0)),
                pl.BlockSpec((blocks, width, rows), lambda j, h: (0, 0, 0)),
                row, row, row, whole,
            ]
            + [whole] * started,
            out_specs=[
                whole,
                pl.BlockSpec((1, chunk), lambda j, h: (0, j)),
                pl.BlockSpec((8, 128), lambda j, h: (0, 0)),
                *share_specs,
            ],
            scratch_shapes=[pltpu.VMEM((rows, tile), jnp.float32)] * 2
            + [pltpu.VMEM((rows, tile), jnp.bfloat16)] * 2
            + [pltpu.VMEM((chunk, width), jnp.bfloat16)]
            + [pltpu.VMEM((width, chunk), jnp.float32)] * coded,
        ),
        out_shape=[
            jax.ShapeDtypeStruct((cells, width), jnp.float32),
            jax.ShapeDtypeStruct((1, count * chunk), jnp.float32),
            jax.ShapeDtypeStruct((8, 128), jnp.float32),
            *share_shapes,
        ],
        compiler_params=params_of(56),
        cost_estimate=pl.CostEstimate(
            flops=10 * cells * count * chunk * width,
            bytes_accessed=2 * cells * count * chunk,
            transcendentals=16 * cells * count * chunk,
        ),
        name="regions",
    )(half, peaks, kept, got, hidden, hidden_t, a, fa, ck, cf, *([before] if started else []))


def outer_kernel(coded, half_ref, x_ref, left_ref, *outs):
    dw_ref = outs[-1]
    tile = min(256, x_ref.shape[1])
    for c in range(0, x_ref.shape[1], tile):
        cols = slice(c, c + tile)
        dw_ref[:, cols] = jnp.dot(left_ref[...], x_ref[:, cols], preferred_element_type=jnp.float32)
    if coded:
        give_shares(half_ref[2], dw_ref, *outs[:3])


def outer(half, peaks, left, first, count, chunk, per_half, coded):
    width, cells = left.shape
    share_specs, share_shapes = share_outputs(width, chunk, count, coded)
    return pl.pallas_call(
        functools.partial(outer_kernel, coded),
        grid_spec=pltpu.PrefetchScalarGridSpec(
            num_scalar_prefetch=1,
            grid=(count,),
            in_specs=[
                pl.BlockSpec((cells, chunk), lambda j, h: (0, h[0] * per_half + first + j)),
                pl.BlockSpec((width, cells), lambda j, h: (0, 0)),
            ],
            out_specs=share_specs,
            scratch_shapes=[pltpu.VMEM((width, chunk), jnp.float32)] * coded,
        ),
        out_shape=share_shapes,
        compiler_params=params_of(48),
        cost_estimate=pl.CostEstimate(
            flops=2 * cells * count * chunk * width, bytes_accessed=2 * cells * count * chunk, transcendentals=0
        ),
        name="outer",
    )(half, peaks, left)


def part_of(values, which, size, axis=0):
    return lax.dynamic_slice_in_dim(values, which * size, size, axis)


def across_cores(values):
    return lax.ppermute(values, "pipe", [(0, 1), (1, 0)])


def shift_of(step, index, count):
    if count & (count - 1) == 0:
        return index ^ step
    return (index + step) % count


def scatter_cells(partial):
    cells = partial.shape[0]
    pipe, mine, count = lax.axis_index("pipe"), lax.axis_index("tensor"), lax.axis_size("tensor")
    half = cells // 2
    got = across_cores(part_of(partial, 1 - pipe, half))
    chip_sum = part_of(partial, pipe, half) + got
    rows = half // count
    pieces = [part_of(chip_sum, mine, rows)]
    for step in range(1, count):
        there = shift_of(step, mine, count)
        route = [(i, shift_of(step, i, count)) for i in range(count)]
        pieces.append(lax.ppermute(part_of(chip_sum, there, rows), "tensor", route))
    return pieces


def gather_cells(own):
    count = lax.axis_size("tensor")
    pieces = [own]
    for step in range(1, count):
        route = [(i, shift_of(step, i, count)) for i in range(count)]
        pieces.append(lax.ppermute(own, "tensor", route))
    return pieces + [across_cores(piece) for piece in pieces]


def rows_at(place_ref, index, count, rows):
    core, mine = place_ref[0], place_ref[1]
    step = index % count
    if count & (count - 1) == 0:
        sender = mine ^ step
    else:
        sender = lax.rem(mine - step + count, jnp.int32(count))
    here = core if index < count else 1 - core
    return (here * count + sender) * rows


def hidden_kernel(count, place_ref, *refs):
    pieces, (wide_ref, turned_ref, all_s) = refs[:-3], refs[-3:]
    rows, width = pieces[0].shape
    for index, piece in enumerate(pieces):
        at = pl.ds(pl.multiple_of(rows_at(place_ref, index, count, rows), 16), rows)
        all_s[at, :] = piece[...].astype(jnp.float32)
    scaled = all_s[...] * (-LOG2E)
    high = scaled.astype(jnp.bfloat16)
    wide_ref[:, :width] = high
    wide_ref[:, width:] = (scaled - high.astype(jnp.float32)).astype(jnp.bfloat16)
    size = turned_ref.shape[2]
    for block in range(turned_ref.shape[0]):
        turned_ref[block] = jnp.transpose(all_s[block * size : (block + 1) * size, :]).astype(jnp.bfloat16)


def left_kernel(count, place_ref, *refs):
    pieces, (left_ref, all_s) = refs[:-2], refs[-2:]
    rows = pieces[0].shape[0]
    for index, piece in enumerate(pieces):
        at = pl.ds(pl.multiple_of(rows_at(place_ref, index, count, rows), 16), rows)
        all_s[at, :] = piece[...].astype(jnp.float32)
    left_ref[...] = jnp.transpose(all_s[...]).astype(jnp.bfloat16)


def assemble(kernel, place, pieces, out_shape, name):
    rows, width = pieces[0].shape
    return one_step(
        functools.partial(kernel, len(pieces) // 2), pieces, out_shape, name, place,
        [pltpu.VMEM((rows * len(pieces), width), jnp.float32)],
    )


def exchange_bits(axis):
    count = lax.axis_size(axis)
    return [1 << i for i in range((count - 1).bit_length())]


def exchanged(values, axis, bit):
    count = lax.axis_size(axis)
    return values + lax.ppermute(values, axis, [(i, i ^ bit) for i in range(count)])


def all_sum(values, axes):
    for axis in axes:
        for bit in exchange_bits(axis):
            values = exchanged(values, axis, bit)
    return values


def join_cores(own):
    other = across_cores(own)
    first = lax.axis_index("pipe") == 0
    return jnp.where(first, own, other), jnp.where(first, other, own)


def body(
    peak_data,
    region_weights,
    out_bias,
    region_factor,
    region_keep,
    cell_factor,
    batch_ids,
    latent_noise,
    enc_bias_in,
    enc_square,
    enc_bias_two,
    enc_heads,
    head_bias,
    dec_first,
    dec_bias_one,
    dec_square,
    dec_bias_two,
):
    cells, regions_local = peak_data.shape
    weight = region_weights[0]
    width = weight.shape[1]
    latent = latent_noise.shape[1]
    batches = dec_first.shape[0] - latent
    window = -(-regions_local // 256) * 128
    overlap = 2 * window - regions_local
    pipe, mine, tensors = lax.axis_index("pipe"), lax.axis_index("tensor"), lax.axis_size("tensor")
    cell_total = cells * lax.axis_size("dp")
    region_total = regions_local * tensors
    norm_scale = float(cell_total) ** (-0.5)

    def of_core(values, core, axis=0):
        return lax.dynamic_slice_in_dim(values, core * (regions_local - window), window, axis)

    keep = of_core(region_keep, pipe).astype(jnp.float32)
    dp_at = lax.axis_index("dp")
    place = jnp.stack([pipe, mine, dp_at]).astype(jnp.int32)
    chunk = next(c for c in (1792, 256, 128) if window % c == 0 and (regions_local - window) % c == 0)
    chunks = window // chunk
    ahead = min(3, chunks - 1) * chunk
    coded = lax.axis_size("dp") == 4 and chunk % 256 == 0
    if overlap:
        mine_alone = (pipe == 0) | (jnp.arange(window) >= overlap)
        keep = jnp.where(mine_alone, keep, 0.0)
        peak_data = of_core(peak_data, pipe, 1)
        own = of_core(weight, pipe)
        got = across_cores(of_core(weight, 1 - pipe))
        kept_enc = got_enc = jnp.where(mine_alone[:, None], jnp.where(pipe == 0, own, got), 0)
        weight = jnp.where(pipe == 0, got, own)
        got_spans = [(weight, 0, 0, chunks)]
        got_parts = [(kept_enc, got_enc, 0, 0, chunks)]
        half = jnp.stack([jnp.zeros_like(place[0]), place[0], place[2]])
    else:
        other_at = (1 - pipe) * (regions_local - window)
        got_first = across_cores(lax.dynamic_slice_in_dim(weight, other_at, ahead, 0))
        got_rest = across_cores(lax.dynamic_slice_in_dim(weight, other_at + ahead, window - ahead, 0))
        got_parts = [(weight, got_first, 0, 0, ahead // chunk), (weight, got_rest, ahead // chunk, 0, chunks - ahead // chunk)]
        cut = ahead // chunk
        middle = cut + (chunks - cut) // 2
        got_spans = [(got_first, 0, 0, cut), (got_rest, 0, cut, middle), (got_rest, middle - cut, middle, chunks)]
        half = jnp.stack([place[0], place[0], place[2]])

    own_rows = cells // (2 * tensors)
    own_at = pipe * tensors + mine
    noise_own = part_of(latent_noise, own_at, own_rows)
    ids_own = part_of(batch_ids[:, None], own_at, own_rows)
    heads_t = jnp.transpose(enc_heads)
    enc = (
        enc_bias_in[None], enc_square, enc_bias_two[None], heads_t[:latent], heads_t[latent:],
        head_bias[None, :latent], head_bias[None, latent:],
    )
    dec = (dec_first[:latent], dec_first[latent:], dec_bias_one[None], dec_square, dec_bias_two[None])

    a = jnp.exp(of_core(out_bias, pipe))[None]
    fa = a * of_core(region_factor, pipe)[None]
    ck = (keep * norm_scale)[None]
    log_fa = jnp.log(fa)
    cf_wide = jnp.broadcast_to(cell_factor[:, None], (cells, 128))
    partial = []
    for kept_w, got_w, first, at, count in got_parts:
        partial = project(half, peak_data, kept_w, got_w, keep[None], log_fa, partial, first, at, count, chunk, chunks)
    partial, seen = partial
    pieces = scatter_cells(partial)
    owed = jnp.sum(seen[:, 0] * (BIG_BITS * LN2 - jnp.log(cell_factor))) - jnp.sum(seen[:, 1:4])
    early = (noise_own, ids_own, enc, dec, a, fa, ck, cf_wide, owed[None, None])
    pieces, early = lax.optimization_barrier((pieces, early))
    noise_own, ids_own, enc, dec, a, fa, ck, cf_wide, owed = early
    summed, z_low, g2_own, kl_sum = one_step(
        functools.partial(forward_kernel, len(pieces)),
        [*pieces, noise_own, ids_own, *enc, *dec],
        [
            jax.ShapeDtypeStruct((own_rows, width), jnp.float32),
            jax.ShapeDtypeStruct((own_rows, latent), jnp.bfloat16),
            jax.ShapeDtypeStruct((own_rows, width), jnp.bfloat16),
            jax.ShapeDtypeStruct((1, 1), jnp.float32),
        ],
        "small_forward",
    )
    rows_b = min(512, cells // 2)
    hidden, hidden_t = assemble(
        hidden_kernel, place, gather_cells(g2_own),
        [
            jax.ShapeDtypeStruct((cells, 2 * width), jnp.bfloat16),
            jax.ShapeDtypeStruct((cells // rows_b, width, rows_b), jnp.bfloat16),
        ],
        "hidden",
    )

    dg2, lines, biases, losses = None, [], [], []
    for got_w, at, first, end in got_spans:
        if len(lines) > 1:
            lines[-2] = line_joined(lines[-2], chunk)
            dg2 = after(dg2, lines[-2][0])
            lines[-2] = line_last(lines[-2])
        dg2, bias, loss, *shares = regions_pass(
            half, peak_data, weight, got_w, hidden, hidden_t, a, fa, ck, cf_wide, dg2, first, at, end - first, chunk,
            chunks, coded,
        )
        dg2 = after(dg2, *[line[0] for line in lines])
        lines.append(line_start(shares))
        biases.append(bias)
        losses.append(loss)
    pieces = scatter_cells(dg2)
    if len(lines) > 1:
        lines[-2] = line_joined(lines[-2], chunk)
        pieces[0] = after(pieces[0], lines[-2][0])
        lines[-2] = line_last(lines[-2])
    grad_shapes = [w.shape for w in ordered(enc + dec)]
    places, pack_rows = pack_places(grad_shapes)
    pack_half = pack_rows // 2
    dp_own, pack = one_step(
        functools.partial(backward_kernel, len(pieces), norm_scale, len(losses)),
        [*pieces, summed, z_low, noise_own, ids_own, *enc, *dec, kl_sum + owed, *losses],
        [
            jax.ShapeDtypeStruct((own_rows, width), jnp.bfloat16),
            jax.ShapeDtypeStruct((pack_rows, width), jnp.float32),
        ],
        "small_backward",
    )
    dp_own = after(dp_own, *[line[0] for line in lines])
    lines[-1] = line_joined(lines[-1], chunk)
    (left,) = assemble(
        left_kernel, place, gather_cells(dp_own), [jax.ShapeDtypeStruct((width, cells), jnp.bfloat16)], "left"
    )
    left = after(left, lines[-1][0])
    lines[-1] = line_last(lines[-1])

    spans = [(first, end) for _, _, first, end in got_spans]
    order = [1, 0, 2][: len(spans)] if len(spans) > 1 else [0]
    enc_lines, under_way = [], []
    for index, (first, end) in enumerate([spans[i] for i in order]):
        if index:
            left = after(left, shares[0])
        if index > 1:
            line = line_joined(under_way.pop(0), chunk)
            left = after(left, line[0])
            enc_lines.append(line_last(line))
        shares = list(outer(half, peak_data, left, first, end - first, chunk, chunks, coded))
        if index == min(1, len(spans) - 1):
            pack = after(pack, *([waiting] if index else []))
            pack = part_of(pack, pipe, pack_half) + across_cores(part_of(pack, 1 - pipe, pack_half))
            steps = [("tensor", bit) for bit in exchange_bits("tensor")]
            while len(steps) > 1:
                pack = exchanged(pack, *steps.pop(0))
            shares[0] = after(shares[0], pack)
        elif index:
            pack = exchanged(pack, *steps.pop(0))
            shares[0] = after(shares[0], pack)
        waiting = shares[0]
        if index:
            beside = [line[0] for line in under_way + enc_lines] + ([lines[-1][0]] if index == 1 else [])
            shares[0] = after(shares[0], *beside)
        under_way.append(line_start(shares))
    for step in steps:
        pack = exchanged(pack, *step)
    sums = jnp.concatenate([pack, jnp.concatenate(biases, axis=1).reshape(-1, 128)], axis=0)
    sums = after(sums, under_way[-1][0])
    joined = []
    for line in under_way:
        if enc_lines:
            line[0] = after(line[0], enc_lines[-1][0])
        line = line_joined(line, chunk)
        joined.append(line[0])
        enc_lines.append(line_last(line))

    dec_own = [line_end(line, chunk) for line in lines]
    dec_got = [lax.ppermute(share, "pipe", [(0, 1)]) for share in dec_own]
    enc_own = [line_end(enc_lines[order.index(i)], chunk) for i in range(len(order))]
    enc_got = [lax.ppermute(share, "pipe", [(1, 0)]) for share in enc_own]
    is_first = pipe == 0
    lower = [jnp.where(is_first, e, d) for e, d in zip(enc_own, dec_got)]
    upper = [jnp.where(is_first, e, d) for e, d in zip(enc_got, dec_own)]
    upper[0] = upper[0][:, overlap:]
    region_grad = jnp.transpose(jnp.concatenate(lower + upper, axis=1))[None]

    sums = after(sums, joined[0])
    for bit in exchange_bits("dp"):
        if bit > 1:
            sums = after(sums, joined[-1], *dec_got)
        sums = exchanged(sums, "dp", bit)
    lower, upper = join_cores(sums)
    bias_grad = jnp.concatenate([lower[pack_half:].reshape(-1), upper[pack_half:].reshape(-1)[overlap:]])
    lower, upper = lower[:pack_half], upper[:pack_half]

    shapes = [w.shape for w in enc + dec]
    ranked = ordered([RankedShape(*shape, index) for index, shape in enumerate(shapes)])
    rows_of = {entry.index: row for row, entry in zip(places, ranked)}
    groups = [(0,), (1,), (2,), (3, 4), (5,), (6,), (7, 8), (9,), (10,), (11,)]
    cuts = [[(rows_of[i], *shapes[i]) for i in group] for group in groups] + [[(pack_rows - 1, 1, 1)]]
    out_shape = [jax.ShapeDtypeStruct((sum(c[1] for c in cut), cut[0][2]), jnp.float32) for cut in cuts]
    (d_bias_in, d_square, d_bias_two, d_heads, d_mean_b, d_var_b, d_first, d_bias_one, d_dec_square, d_dec_bias_two,
     loss_total) = one_step(
        functools.partial(unpack_kernel, cuts), [lower, upper], out_shape, "unpack", None,
        [pltpu.VMEM((pack_rows, width), jnp.float32)],
    )
    mean_loss = loss_total[0, 0] / (cell_total * region_total)
    return (
        region_grad,
        bias_grad,
        d_bias_in[0],
        d_square,
        d_bias_two[0],
        jnp.transpose(d_heads),
        jnp.concatenate([d_mean_b[0], d_var_b[0]], axis=0),
        d_first,
        d_bias_one[0],
        d_dec_square,
        d_dec_bias_two[0],
        mean_loss,
    )


def solution(mesh):
    in_specs = (
        P("dp", "tensor"),
        P("pipe", "tensor", None),
        P("tensor"),
        P("tensor"),
        P("tensor"),
        P("dp"),
        P("dp"),
        P("dp", None),
        *[P()] * 9,
    )
    out_specs = (P("pipe", "tensor", "dp"), P("tensor"), *[P()] * 10)
    return jax.shard_map(body, mesh=mesh, in_specs=in_specs, out_specs=out_specs, check_vma=False)
```

```python
import functools

import jax
import jax.numpy as jnp
import numpy as np
from jax import lax
from jax.experimental import pallas as pl
from jax.experimental.pallas import tpu as pltpu
from jax.sharding import PartitionSpec as P

EXACT = lax.Precision.HIGHEST
NORM_EPS = 1e-05
LOG2E = float(np.log2(np.e))
LN2 = float(np.log(2.0))
BIG_BITS = 56
BIG = float(2.0**BIG_BITS)
MIB = 1 << 20


def params_of(mib):
    return pltpu.CompilerParams(vmem_limit_bytes=mib * MIB)


def layer_norm(values):
    centred = values - jnp.mean(values, axis=-1, keepdims=True)
    return centred * lax.rsqrt(jnp.mean(centred * centred, axis=-1, keepdims=True) + NORM_EPS)


def silu(values):
    return values * jax.nn.sigmoid(values)


def mm(a, b):
    return lax.dot_general(a, b, (((1,), (0,)), ((), ())), precision=EXACT, preferred_element_type=jnp.float32)


def mm_t(a, b):
    return lax.dot_general(a, b, (((1,), (1,)), ((), ())), precision=EXACT, preferred_element_type=jnp.float32)


def encoder_small(summed, bias_in, square, bias_two, mean_w, var_w, mean_b, var_b, noise_rows):
    hidden = silu(layer_norm(summed + bias_in))
    hidden = silu(layer_norm(mm(hidden, square) + bias_two))
    average = mm_t(hidden, mean_w) + mean_b
    variance = jnp.exp(mm_t(hidden, var_w) + var_b) + 0.0001
    sample = average + jnp.sqrt(variance) * noise_rows
    kl_rows = 0.5 * jnp.sum(average * average + variance - jnp.log(variance) - 1.0, axis=1, keepdims=True)
    return (sample, jnp.sum(kl_rows, axis=0, keepdims=True))


def decoder_small(latent_rows, onehot, first_z, first_b, bias_one, square, bias_two):
    hidden = silu(layer_norm(mm(latent_rows, first_z) + mm(onehot, first_b) + bias_one))
    return silu(layer_norm(mm(hidden, square) + bias_two))


def onehot_of(ids, width):
    codes = lax.broadcasted_iota(jnp.int32, (ids.shape[0], width), 1)
    return (ids == codes).astype(jnp.float32)


def forward_kernel(count, *refs):
    parts = refs[:count]
    noise, ids = refs[count : count + 2]
    enc = [r[...] for r in refs[count + 2 : count + 9]]
    dec = [r[...] for r in refs[count + 9 : count + 14]]
    summed_out, z_out, g2_out, kl_out = refs[count + 14 :]
    summed = parts[0][...]
    for part in parts[1:]:
        summed = summed + part[...]
    sample, kl_sum = encoder_small(summed, *enc, noise[...])
    z_low = sample.astype(jnp.bfloat16)
    hidden = decoder_small(z_low.astype(jnp.float32), onehot_of(ids[...], dec[1].shape[0]), *dec)
    summed_out[...] = summed
    z_out[...] = z_low
    g2_out[...] = hidden.astype(jnp.bfloat16)
    kl_out[...] = kl_sum


def pack_places(shapes):
    places, row = [], 0
    for rows, _ in shapes:
        places.append(row)
        row += rows if rows == 1 else -(-rows // 8) * 8
    return places, -(-(row + 1) // 16) * 16


def backward_kernel(count, norm_scale, calls, *refs):
    parts = refs[:count]
    summed, z_low, noise, ids = refs[count : count + 4]
    enc = [r[...] for r in refs[count + 4 : count + 11]]
    dec = [r[...] for r in refs[count + 11 : count + 16]]
    owed = refs[count + 16]
    losses = refs[count + 17 : count + 17 + calls]
    dp_out, pack_out = refs[count + 17 + calls :]
    dg2 = parts[0][...]
    for part in parts[1:]:
        dg2 = dg2 + part[...]
    onehot = onehot_of(ids[...], dec[1].shape[0])
    unused, pull = jax.vjp(lambda z, *w: decoder_small(z, onehot, *w), z_low[...].astype(jnp.float32), *dec)
    dz, *dec_grads = pull(dg2)
    noise_rows = noise[...]
    unused, pull = jax.vjp(lambda s, *w: encoder_small(s, *w, noise_rows), summed[...], *enc)
    dz_low = dz.astype(jnp.bfloat16).astype(jnp.float32)
    dp, *enc_grads = pull((dz_low, jnp.full((1, 1), norm_scale, jnp.float32)))
    dp_out[...] = dp.astype(jnp.bfloat16)
    pack_out[...] = jnp.zeros_like(pack_out)
    grads = ordered(enc_grads + dec_grads)
    for row, grad in zip(pack_places([g.shape for g in grads])[0], grads):
        pack_out[row : row + grad.shape[0], : grad.shape[1]] = grad
    loss = losses[0][...]
    for ref in losses[1:]:
        loss = loss + ref[...]
    loss = jnp.sum(jnp.sum(loss, axis=0, keepdims=True), axis=1, keepdims=True) * (LN2 / norm_scale) + owed[...]
    pack_out[pack_out.shape[0] - 1 :, 0:1] = loss


def unpack_kernel(cuts, lower_ref, upper_ref, *refs):
    pack = refs[-1]
    half = lower_ref.shape[0]
    pack[:half, :] = lower_ref[...]
    pack[half:, :] = upper_ref[...]
    for cut, out in zip(cuts, refs[:-1]):
        at = 0
        for row, rows, columns in cut:
            out[at : at + rows, :] = pack[row : row + rows, :columns]
            at += rows


class RankedShape:
    def __init__(self, rows, columns, index):
        self.shape, self.index = (rows, columns), index


def ordered(values):
    return [v for v in values if v.shape[0] > 1] + [v for v in values if v.shape[0] == 1]


STRIP = 16
TOP = 32767.0


def coded_rows(share, chunk):
    return chunk // 256 * share + STRIP


def code(values, out_ref, base, tile, share, strip):
    largest = jnp.maximum(jnp.max(jnp.abs(values), axis=0, keepdims=True), 1e-30)
    level = jnp.ceil(jnp.log2(largest) * 64.0 + 0.01)
    scaled = values * (TOP * jnp.exp2(level * (-1.0 / 64.0)))
    at = base + tile * share
    out_ref[at : at + share, :] = jnp.floor(scaled + 0.5).astype(jnp.int32).astype(jnp.int16)
    row = lax.broadcasted_iota(jnp.int32, (STRIP, 256), 0)
    return jnp.where(row == tile, level, strip)


def code_all(parts, out_ref, base, share):
    strip = jnp.zeros((STRIP, 256), jnp.float32)
    for tile, values in enumerate(parts):
        strip = code(values, out_ref, base, tile, share, strip)
    at = base + len(parts) * share
    out_ref[at : at + STRIP, :] = strip.astype(jnp.int32).astype(jnp.int16)


def decode(in_ref, base, tiles, share, tile):
    at = base + tiles * share
    level = in_ref[at : at + STRIP, :].astype(jnp.int32).astype(jnp.float32)[tile : tile + 1, :]
    at = base + tile * share
    values = in_ref[at : at + share, :].astype(jnp.int32).astype(jnp.float32)
    return values * (jnp.exp2(level * (1.0 / 64.0)) * (1.0 / TOP))


def give_shares(z, dw_ref, sent_ref, own_ref, other_ref):
    share, chunk = own_ref.shape

    def rows(which):
        return pl.ds(pl.multiple_of(which * share, 16), share)

    for place, which in enumerate((z ^ 1, z ^ 3)):
        parts = [dw_ref[rows(which), c : c + 256] for c in range(0, chunk, 256)]
        code_all(parts, sent_ref, place * coded_rows(share, chunk), share)
    own_ref[...] = dw_ref[rows(z), :]
    other_ref[...] = dw_ref[rows(z ^ 2), :]


def share_outputs(width, chunk, count, coded):
    if not coded:
        return [pl.BlockSpec((width, chunk), lambda j, h: (0, j))], [jax.ShapeDtypeStruct((width, count * chunk), jnp.float32)]
    share = width // 4
    rows = 2 * coded_rows(share, chunk)
    specs = [pl.BlockSpec((rows, 256), lambda j, h: (j, 0))] + [pl.BlockSpec((share, chunk), lambda j, h: (0, j))] * 2
    shapes = [jax.ShapeDtypeStruct((count * rows, 256), jnp.int16)]
    return specs, shapes + [jax.ShapeDtypeStruct((share, count * chunk), jnp.float32)] * 2


def join_kernel(got_ref, own_ref, other_ref, sent_ref, sum_ref, *, chunk):
    share, width = own_ref.shape
    tiles, rows = chunk // 256, coded_rows(share, chunk)
    for j in range(width // chunk):
        parts = []
        for tile in range(tiles):
            cols = slice(j * chunk + tile * 256, j * chunk + tile * 256 + 256)
            sum_ref[:, cols] = own_ref[:, cols] + decode(got_ref, 2 * j * rows, tiles, share, tile)
            parts.append(other_ref[:, cols] + decode(got_ref, (2 * j + 1) * rows, tiles, share, tile))
        code_all(parts, sent_ref, j * rows, share)


def total_kernel(sum_ref, got_ref, out_ref, *, chunk):
    share, width = sum_ref.shape
    tiles, rows = chunk // 256, coded_rows(share, chunk)
    for j in range(width // chunk):
        for tile in range(tiles):
            cols = slice(j * chunk + tile * 256, j * chunk + tile * 256 + 256)
            out_ref[:, cols] = sum_ref[:, cols] + decode(got_ref, j * rows, tiles, share, tile)


def one_step(kernel, args, out_shape, name, place=None, scratch=()):
    def whole(array):
        return pl.BlockSpec(array.shape, lambda i, rank=len(array.shape): (0,) * rank)

    front = [] if place is None else [place]
    return pl.pallas_call(
        kernel,
        grid=(1,),
        in_specs=[pl.BlockSpec(memory_space=pltpu.SMEM)] * len(front) + [whole(x) for x in args],
        out_specs=[whole(x) for x in out_shape],
        out_shape=list(out_shape),
        scratch_shapes=list(scratch),
        compiler_params=params_of(48),
        name=name,
    )(*front, *args)


def line_start(pieces):
    if len(pieces) == 1:
        return [lax.psum_scatter(pieces[0], "dp", scatter_dimension=0, tiled=True)]
    return [lax.ppermute(pieces[0], "dp", [(i, i ^ 1) for i in range(4)]), *pieces[1:]]


def line_joined(state, chunk):
    if len(state) == 1:
        return state
    got, own, other = state
    sent = jax.ShapeDtypeStruct((got.shape[0] // 2, 256), jnp.int16)
    kernel = functools.partial(join_kernel, chunk=chunk)
    return one_step(kernel, state, [sent, jax.ShapeDtypeStruct(own.shape, jnp.float32)], "join")


def line_last(state):
    if len(state) == 1:
        return state
    return [lax.ppermute(state[0], "dp", [(i, i ^ 2) for i in range(4)]), state[1]]


def line_end(state, chunk):
    if len(state) == 1:
        return state[0]
    got, own = state
    kernel = functools.partial(total_kernel, chunk=chunk)
    return one_step(kernel, [own, got], [jax.ShapeDtypeStruct(own.shape, jnp.float32)], "total")[0]


def after(value, *others):
    return lax.optimization_barrier((value, *others))[0]


def chosen(core, encoder, kept_ref, got_ref):
    own = core == (0 if encoder else 1)
    return jnp.where(own, kept_ref[...], got_ref[...])


def weight_specs(chunk, width, per_half, first, got_first, encoder):
    owner = 0 if encoder else 1

    def kept(j, h):
        return (jnp.where(h[1] == owner, h[0] * per_half + first + j, 0), 0)

    def got(j, h):
        return (jnp.where(h[1] == owner, 0, got_first + j), 0)

    return [pl.BlockSpec((chunk, width), kept), pl.BlockSpec((chunk, width), got)]


def project_kernel(started, half_ref, x_ref, kept_ref, got_ref, bias_ref, factor_ref, keep_ref, *refs):
    out_ref, seen_ref = refs[-2:]
    chunk, width = kept_ref.shape
    keep = keep_ref[...]
    row = lax.broadcasted_iota(jnp.int32, (width, chunk), 0)
    terms = jnp.where(row == 0, keep, 0.0)
    rest = keep * (bias_ref[...] + jnp.log(factor_ref[...]))
    for place in range(1, 4):
        high = rest.astype(jnp.bfloat16).astype(jnp.float32)
        terms = jnp.where(row == place, high, terms)
        rest = rest - high
    right = jnp.concatenate([chosen(half_ref[1], True, kept_ref, got_ref), jnp.transpose(terms).astype(jnp.bfloat16)], axis=1)
    part = jnp.dot(x_ref[...], right, preferred_element_type=jnp.float32)

    @pl.when(pl.program_id(0) == 0)
    def first():
        out_ref[...] = part[:, :width] + refs[0][...] if started else part[:, :width]
        seen_ref[...] = part[:, width:] + refs[1][...] if started else part[:, width:]

    @pl.when(pl.program_id(0) != 0)
    def later():
        out_ref[...] += part[:, :width]
        seen_ref[...] += part[:, width:]


def project(half, peaks, kept, got, region_rows, before, first, got_first, count, chunk, per_half):
    cells, width = peaks.shape[0], kept.shape[1]
    whole = pl.BlockSpec((cells, width), lambda j, h: (0, 0))
    row = pl.BlockSpec((1, chunk), lambda j, h: (0, h[0] * per_half + first + j))
    return pl.pallas_call(
        functools.partial(project_kernel, bool(before)),
        grid_spec=pltpu.PrefetchScalarGridSpec(
            num_scalar_prefetch=1,
            grid=(count,),
            in_specs=[
                pl.BlockSpec((cells, chunk), lambda j, h: (0, h[0] * per_half + first + j)),
                *weight_specs(chunk, width, per_half, first, got_first, True),
                row,
                row,
                row,
            ]
            + [whole] * len(before),
            out_specs=[whole, whole],
        ),
        out_shape=[jax.ShapeDtypeStruct((cells, width), jnp.float32)] * 2,
        compiler_params=params_of(48),
        cost_estimate=pl.CostEstimate(
            flops=2 * cells * count * chunk * width, bytes_accessed=2 * cells * count * chunk, transcendentals=0
        ),
        name="project",
    )(half, peaks, kept, got, *region_rows, *before)


def regions_kernel(
    tile, rows_at_once, piece, norm_scale, cut, started, coded, half_ref, x_ref, kept_ref, got_ref, rest_ref, g_ref, gt_ref, bias_in_ref, factor_ref, keep_ref,
    cf_ref, *refs,
):
    outs = refs[1 if started else 0 :]
    dg_ref, bias_ref, loss_ref = outs[:3]
    m0, m1, e0, e1, w_ref, dw_ref = outs[-6:] if coded else (*outs[4:], outs[3])
    cells, chunk = x_ref.shape
    blocks = cells // rows_at_once
    M, E = (m0, m1), (e0, e1)

    got = jnp.where(pl.program_id(0) < cut, got_ref[...], rest_ref[...])
    w_ref[...] = jnp.where(half_ref[1] == 1, kept_ref[...], got)

    @pl.when(pl.program_id(0) == 0)
    def first():
        dg_ref[...] = refs[0][...] if started else jnp.zeros_like(dg_ref)
        loss_ref[...] = jnp.zeros_like(loss_ref)

    def one_tile(t, carry):
        cols = pl.ds(pl.multiple_of(t * tile, 128), tile)
        w = w_ref[cols, :]
        w2 = jnp.concatenate([w, w], axis=1)
        wide = (8, tile)
        bias_row = jnp.exp(bias_in_ref[:, cols])
        a = jnp.broadcast_to(bias_row, wide)[None]
        fa = jnp.broadcast_to(bias_row * factor_ref[:, cols], wide)[None]
        ck = jnp.broadcast_to(keep_ref[:, cols] * norm_scale, wide)[None]

        def rows(i, o=0, n=rows_at_once):
            return pl.ds(pl.multiple_of(i * rows_at_once + o, 16), n)

        def logit(i, s, o, n):
            M[s][o : o + n, :] = lax.dot_general(
                g_ref[rows(i, o, n), :], w2, (((1,), (1,)), ((), ())), preferred_element_type=jnp.float32
            )

        def elementwise(i, s, o, sums):
            e_sum, l_sum = sums
            shape = (piece // 8, 8, tile)
            u = jnp.exp2(M[s][o : o + piece, :]).reshape(shape)
            cf = cf_ref[rows(i, o, piece), :]
            cf = jnp.concatenate([cf] * (tile // 128), axis=1).reshape(shape)
            seen = (x_ref[rows(i, o, piece), cols] * jnp.bfloat16(BIG)).astype(jnp.float32).reshape(shape)
            total = u + a
            rest = (total - fa * cf) + seen
            d = pltpu.reciprocal(rest, approx=True)
            slope = (u * ck) * (d - pltpu.reciprocal(total, approx=True))
            ratio = (d * total).reshape(piece // 16, 2, 8, tile)
            E[s][o : o + piece, :] = slope.reshape(piece, tile).astype(jnp.bfloat16)
            e_sum = e_sum + jnp.sum(slope, axis=0)
            l_sum = l_sum + jnp.sum(jnp.log2(ratio[:, 0] * ratio[:, 1]), axis=0)
            return e_sum, l_sum

        def cell_grad(i, s):
            dg_ref[rows(i), :] += jnp.dot(E[s][...], w, preferred_element_type=jnp.float32)

        def region_grad(i, s, start=False):
            part = jnp.dot(gt_ref[i], E[s][...], preferred_element_type=jnp.float32)
            if start:
                dw_ref[:, cols] = part
            else:
                dw_ref[:, cols] += part

        def step(i, s, sums, logits=True, grads=True, start=False):
            if logits:
                logit(i + 1, 1 - s, 0, rows_at_once)
            for o in range(0, rows_at_once, piece):
                sums = elementwise(i, s, o, sums)
                if grads and o == rows_at_once // 2:
                    cell_grad(i - 1, 1 - s)
            if grads:
                region_grad(i - 1, 1 - s, start)
            return sums

        zero = jnp.zeros(wide, jnp.float32)
        sums = (zero, zero)
        logit(0, 0, 0, rows_at_once)
        sums = step(0, 0, sums, grads=False)
        for i in range(1, blocks):
            sums = step(i, i % 2, sums, logits=i < blocks - 1, start=i == 1)
        cell_grad(blocks - 1, (blocks - 1) % 2)
        region_grad(blocks - 1, (blocks - 1) % 2, blocks == 1)
        bias_ref[:, cols] = jnp.sum(sums[0], axis=0, keepdims=True)
        kept = sums[1] * ck[0]
        for c in range(0, tile, 128):
            loss_ref[...] += kept[:, c : c + 128]
        return carry

    lax.fori_loop(0, chunk // tile, one_tile, 0)
    if coded:
        give_shares(half_ref[2], dw_ref, *outs[3:6])


def regions_pass(norm_scale, half, peaks, kept, got_pair, hidden, hidden_t, region_rows, cf, before, first, count, chunk, per_half, coded):
    cells, width = peaks.shape[0], kept.shape[1]
    blocks, _, rows = hidden_t.shape
    tile, piece = min(256, chunk), 64
    cut = got_pair[0].shape[0] // chunk
    started = before is not None
    whole = pl.BlockSpec((cells, width), lambda j, h: (0, 0))
    row = pl.BlockSpec((1, chunk), lambda j, h: (0, h[0] * per_half + first + j))
    share_specs, share_shapes = share_outputs(width, chunk, count, coded)
    return pl.pallas_call(
        functools.partial(regions_kernel, tile, rows, piece, norm_scale, cut - first, started, coded),
        grid_spec=pltpu.PrefetchScalarGridSpec(
            num_scalar_prefetch=1,
            grid=(count,),
            in_specs=[
                pl.BlockSpec((cells, chunk), lambda j, h: (0, h[0] * per_half + first + j)),
                *weight_specs(chunk, width, per_half, first, first, False)[:1],
                pl.BlockSpec((chunk, width), lambda j, h: (jnp.where(h[1] == 1, 0, jnp.minimum(first + j, cut - 1)), 0)),
                pl.BlockSpec((chunk, width), lambda j, h: (jnp.where(h[1] == 1, 0, jnp.maximum(first + j - cut, 0)), 0)),
                pl.BlockSpec((cells, 2 * width), lambda j, h: (0, 0)),
                pl.BlockSpec((blocks, width, rows), lambda j, h: (0, 0, 0)),
                row, row, row, whole,
            ]
            + [whole] * started,
            out_specs=[
                whole,
                pl.BlockSpec((1, chunk), lambda j, h: (0, j)),
                pl.BlockSpec((8, 128), lambda j, h: (0, 0)),
                *share_specs,
            ],
            scratch_shapes=[pltpu.VMEM((rows, tile), jnp.float32)] * 2
            + [pltpu.VMEM((rows, tile), jnp.bfloat16)] * 2
            + [pltpu.VMEM((chunk, width), jnp.bfloat16)]
            + [pltpu.VMEM((width, chunk), jnp.float32)] * coded,
        ),
        out_shape=[
            jax.ShapeDtypeStruct((cells, width), jnp.float32),
            jax.ShapeDtypeStruct((1, count * chunk), jnp.float32),
            jax.ShapeDtypeStruct((8, 128), jnp.float32),
            *share_shapes,
        ],
        compiler_params=params_of(56),
        cost_estimate=pl.CostEstimate(
            flops=10 * cells * count * chunk * width,
            bytes_accessed=2 * cells * count * chunk,
            transcendentals=16 * cells * count * chunk,
        ),
        name="regions",
    )(half, peaks, kept, *got_pair, hidden, hidden_t, *region_rows, cf, *([before] if started else []))


def outer_kernel(coded, half_ref, x_ref, left_ref, *outs):
    dw_ref = outs[-1]
    tile = min(256, x_ref.shape[1])
    for c in range(0, x_ref.shape[1], tile):
        cols = slice(c, c + tile)
        dw_ref[:, cols] = jnp.dot(left_ref[...], x_ref[:, cols], preferred_element_type=jnp.float32)
    if coded:
        give_shares(half_ref[2], dw_ref, *outs[:3])


def outer(half, peaks, left, first, count, chunk, per_half, coded):
    width, cells = left.shape
    share_specs, share_shapes = share_outputs(width, chunk, count, coded)
    return pl.pallas_call(
        functools.partial(outer_kernel, coded),
        grid_spec=pltpu.PrefetchScalarGridSpec(
            num_scalar_prefetch=1,
            grid=(count,),
            in_specs=[
                pl.BlockSpec((cells, chunk), lambda j, h: (0, h[0] * per_half + first + j)),
                pl.BlockSpec((width, cells), lambda j, h: (0, 0)),
            ],
            out_specs=share_specs,
            scratch_shapes=[pltpu.VMEM((width, chunk), jnp.float32)] * coded,
        ),
        out_shape=share_shapes,
        compiler_params=params_of(48),
        cost_estimate=pl.CostEstimate(
            flops=2 * cells * count * chunk * width, bytes_accessed=2 * cells * count * chunk, transcendentals=0
        ),
        name="outer",
    )(half, peaks, left)


def part_of(values, which, size, axis=0):
    return lax.dynamic_slice_in_dim(values, which * size, size, axis)


def across_cores(values):
    return lax.ppermute(values, "pipe", [(0, 1), (1, 0)])


def shift_of(step, index, count):
    if count & (count - 1) == 0:
        return index ^ step
    return (index + step) % count


def scatter_cells(partial):
    cells = partial.shape[0]
    pipe, mine, count = lax.axis_index("pipe"), lax.axis_index("tensor"), lax.axis_size("tensor")
    half = cells // 2
    got = across_cores(part_of(partial, 1 - pipe, half))
    chip_sum = part_of(partial, pipe, half) + got
    rows = half // count
    pieces = [part_of(chip_sum, mine, rows)]
    for step in range(1, count):
        there = shift_of(step, mine, count)
        route = [(i, shift_of(step, i, count)) for i in range(count)]
        pieces.append(lax.ppermute(part_of(chip_sum, there, rows), "tensor", route))
    return pieces


def gather_cells(own):
    count = lax.axis_size("tensor")
    pieces = [own]
    for step in range(1, count):
        route = [(i, shift_of(step, i, count)) for i in range(count)]
        pieces.append(lax.ppermute(own, "tensor", route))
    return pieces + [across_cores(piece) for piece in pieces]


def rows_at(place_ref, index, count, rows):
    core, mine = place_ref[0], place_ref[1]
    step = index % count
    if count & (count - 1) == 0:
        sender = mine ^ step
    else:
        sender = lax.rem(mine - step + count, jnp.int32(count))
    here = core if index < count else 1 - core
    return (here * count + sender) * rows


def hidden_kernel(count, place_ref, *refs):
    pieces, (wide_ref, turned_ref, all_s) = refs[:-3], refs[-3:]
    rows, width = pieces[0].shape
    for index, piece in enumerate(pieces):
        at = pl.ds(pl.multiple_of(rows_at(place_ref, index, count, rows), 16), rows)
        all_s[at, :] = piece[...].astype(jnp.float32)
    scaled = all_s[...] * (-LOG2E)
    high = scaled.astype(jnp.bfloat16)
    wide_ref[:, :width] = high
    wide_ref[:, width:] = (scaled - high.astype(jnp.float32)).astype(jnp.bfloat16)
    size = turned_ref.shape[2]
    for block in range(turned_ref.shape[0]):
        turned_ref[block] = jnp.transpose(all_s[block * size : (block + 1) * size, :]).astype(jnp.bfloat16)


def left_kernel(count, place_ref, *refs):
    pieces, (left_ref, all_s) = refs[:-2], refs[-2:]
    rows = pieces[0].shape[0]
    for index, piece in enumerate(pieces):
        at = pl.ds(pl.multiple_of(rows_at(place_ref, index, count, rows), 16), rows)
        all_s[at, :] = piece[...].astype(jnp.float32)
    left_ref[...] = jnp.transpose(all_s[...]).astype(jnp.bfloat16)


def assemble(kernel, place, pieces, out_shape, name):
    rows, width = pieces[0].shape
    return one_step(
        functools.partial(kernel, len(pieces) // 2), pieces, out_shape, name, place,
        [pltpu.VMEM((rows * len(pieces), width), jnp.float32)],
    )


def exchange_bits(axis):
    count = lax.axis_size(axis)
    return [1 << i for i in range((count - 1).bit_length())]


def exchanged(values, axis, bit):
    count = lax.axis_size(axis)
    return values + lax.ppermute(values, axis, [(i, i ^ bit) for i in range(count)])


def all_sum(values, axes):
    for axis in axes:
        for bit in exchange_bits(axis):
            values = exchanged(values, axis, bit)
    return values


def join_cores(own):
    other = across_cores(own)
    first = lax.axis_index("pipe") == 0
    return jnp.where(first, own, other), jnp.where(first, other, own)


def body(
    peak_data,
    region_weights,
    out_bias,
    region_factor,
    region_keep,
    cell_factor,
    batch_ids,
    latent_noise,
    enc_bias_in,
    enc_square,
    enc_bias_two,
    enc_heads,
    head_bias,
    dec_first,
    dec_bias_one,
    dec_square,
    dec_bias_two,
):
    cells, regions_local = peak_data.shape
    weight = region_weights[0]
    width = weight.shape[1]
    latent = latent_noise.shape[1]
    batches = dec_first.shape[0] - latent
    window = -(-regions_local // 256) * 128
    overlap = 2 * window - regions_local
    pipe, mine, tensors = lax.axis_index("pipe"), lax.axis_index("tensor"), lax.axis_size("tensor")
    cell_total = cells * lax.axis_size("dp")
    region_total = regions_local * tensors
    norm_scale = float(cell_total) ** (-0.5)

    def of_core(values, core, axis=0):
        return lax.dynamic_slice_in_dim(values, core * (regions_local - window), window, axis)

    region_rows = [out_bias, region_factor, region_keep.astype(jnp.float32)]
    dp_at = lax.axis_index("dp")
    place = jnp.stack([pipe, mine, dp_at]).astype(jnp.int32)
    chunk = next(c for c in (1792, 256, 128) if window % c == 0 and (regions_local - window) % c == 0)
    chunks = window // chunk
    ahead = min(2, chunks - 1) * chunk
    coded = lax.axis_size("dp") == 4 and chunk % 256 == 0
    if overlap:
        mine_alone = (pipe == 0) | (jnp.arange(window) >= overlap)
        region_rows = [of_core(row, pipe) for row in region_rows]
        region_rows[2] = jnp.where(mine_alone, region_rows[2], 0.0)
        peak_data = of_core(peak_data, pipe, 1)
        own = of_core(weight, pipe)
        got = across_cores(of_core(weight, 1 - pipe))
        kept_enc = got_enc = jnp.where(mine_alone[:, None], jnp.where(pipe == 0, own, got), 0)
        weight = jnp.where(pipe == 0, got, own)
        got_pair, got_spans = (weight, weight), [(0, chunks)]
        got_parts = [(kept_enc, got_enc, 0, 0, chunks)]
        half = jnp.stack([jnp.zeros_like(place[0]), place[0], place[2]])
    else:
        other_at = (1 - pipe) * (regions_local - window)
        got_first = across_cores(lax.dynamic_slice_in_dim(weight, other_at, ahead, 0))
        got_rest = across_cores(lax.dynamic_slice_in_dim(weight, other_at + ahead, window - ahead, 0))
        got_parts = [(weight, got_first, 0, 0, ahead // chunk), (weight, got_rest, ahead // chunk, 0, chunks - ahead // chunk)]
        cut = ahead // chunk
        most = -(-chunks * 4 // 7)
        got_pair, got_spans = (got_first, got_rest), [(0, most), (most, chunks)]
        half = jnp.stack([place[0], place[0], place[2]])

    own_rows = cells // (2 * tensors)
    own_at = pipe * tensors + mine
    noise_own = part_of(latent_noise, own_at, own_rows)
    ids_own = part_of(batch_ids[:, None], own_at, own_rows)
    heads_t = jnp.transpose(enc_heads)
    enc = (
        enc_bias_in[None], enc_square, enc_bias_two[None], heads_t[:latent], heads_t[latent:],
        head_bias[None, :latent], head_bias[None, latent:],
    )
    dec = (dec_first[:latent], dec_first[latent:], dec_bias_one[None], dec_square, dec_bias_two[None])

    region_rows = [row[None] for row in region_rows]
    cf_wide = jnp.broadcast_to(cell_factor[:, None], (cells, 128))
    partial = []
    for kept_w, got_w, first, at, count in got_parts:
        partial = project(half, peak_data, kept_w, got_w, region_rows, partial, first, at, count, chunk, chunks)
    partial, seen = partial
    pieces = scatter_cells(partial)
    owed = jnp.sum(seen[:, 0] * (BIG_BITS * LN2 - jnp.log(cell_factor))) - jnp.sum(seen[:, 1:4])
    early = (noise_own, ids_own, enc, dec, cf_wide, owed[None, None])
    pieces, early = lax.optimization_barrier((pieces, early))
    noise_own, ids_own, enc, dec, cf_wide, owed = early
    summed, z_low, g2_own, kl_sum = one_step(
        functools.partial(forward_kernel, len(pieces)),
        [*pieces, noise_own, ids_own, *enc, *dec],
        [
            jax.ShapeDtypeStruct((own_rows, width), jnp.float32),
            jax.ShapeDtypeStruct((own_rows, latent), jnp.bfloat16),
            jax.ShapeDtypeStruct((own_rows, width), jnp.bfloat16),
            jax.ShapeDtypeStruct((1, 1), jnp.float32),
        ],
        "small_forward",
    )
    rows_b = min(512, cells // 2)
    hidden, hidden_t = assemble(
        hidden_kernel, place, gather_cells(g2_own),
        [
            jax.ShapeDtypeStruct((cells, 2 * width), jnp.bfloat16),
            jax.ShapeDtypeStruct((cells // rows_b, width, rows_b), jnp.bfloat16),
        ],
        "hidden",
    )

    dg2, lines, biases, losses = None, [], [], []
    for first, end in got_spans:
        if len(lines) > 1:
            lines[-2] = line_joined(lines[-2], chunk)
            dg2 = after(dg2, lines[-2][0])
            lines[-2] = line_last(lines[-2])
        dg2, bias, loss, *shares = regions_pass(
            norm_scale, half, peak_data, weight, got_pair, hidden, hidden_t, region_rows, cf_wide, dg2, first,
            end - first, chunk, chunks, coded,
        )
        dg2 = after(dg2, *[line[0] for line in lines])
        lines.append(line_start(shares))
        biases.append(bias)
        losses.append(loss)
    pieces = scatter_cells(dg2)
    if len(lines) > 1:
        lines[-2] = line_joined(lines[-2], chunk)
        pieces[0] = after(pieces[0], lines[-2][0])
        lines[-2] = line_last(lines[-2])
    grad_shapes = [w.shape for w in ordered(enc + dec)]
    places, pack_rows = pack_places(grad_shapes)
    pack_half = pack_rows // 2
    dp_own, pack = one_step(
        functools.partial(backward_kernel, len(pieces), norm_scale, len(losses)),
        [*pieces, summed, z_low, noise_own, ids_own, *enc, *dec, kl_sum + owed, *losses],
        [
            jax.ShapeDtypeStruct((own_rows, width), jnp.bfloat16),
            jax.ShapeDtypeStruct((pack_rows, width), jnp.float32),
        ],
        "small_backward",
    )
    gathered = gather_cells(dp_own)
    lines[-1][0] = after(lines[-1][0], gathered[-1])
    lines[-1] = line_joined(lines[-1], chunk)
    (left,) = assemble(left_kernel, place, gathered, [jax.ShapeDtypeStruct((width, cells), jnp.bfloat16)], "left")
    left = after(left, *[line[0] for line in lines])
    lines[-1] = line_last(lines[-1])

    first, second = max(1, chunks * 2 // 7), max(2, chunks * 5 // 7)
    spans = [(0, first), (first, second), (second, chunks)] if chunks > 2 else [(0, chunks)]
    order = list(range(len(spans)))
    enc_lines, under_way = [], []
    for index, (first, end) in enumerate([spans[i] for i in order]):
        if index:
            left = after(left, shares[0])
        if index > 1:
            line = line_joined(under_way.pop(0), chunk)
            left = after(left, line[0], pack)
            enc_lines.append(line_last(line))
        shares = list(outer(half, peak_data, left, first, end - first, chunk, chunks, coded))
        if index == min(1, len(spans) - 1):
            pack = after(pack, *([waiting] if index else []))
            pack = part_of(pack, pipe, pack_half) + across_cores(part_of(pack, 1 - pipe, pack_half))
            steps = [("tensor", bit) for bit in exchange_bits("tensor")]
            while len(steps) > 1:
                pack = exchanged(pack, *steps.pop(0))
        elif index:
            pack = exchanged(pack, *steps.pop(0))
            shares[0] = after(shares[0], pack)
        waiting = shares[0]
        beside = [line[0] for line in under_way + enc_lines] + ([] if index else [lines[-1][0]])
        shares[0] = after(shares[0], *beside)
        under_way.append(line_start(shares))
    for step in steps:
        pack = exchanged(pack, *step)
    sums = jnp.concatenate([pack, jnp.concatenate(biases, axis=1).reshape(-1, 128)], axis=0)
    sums = after(sums, under_way[-1][0])
    joined = []
    for line in under_way:
        line = line_joined(line, chunk)
        joined.append(line[0])
        enc_lines.append(line_last(line))

    dec_own = [line_end(line, chunk) for line in lines]
    dec_got = [lax.ppermute(share, "pipe", [(0, 1)]) for share in dec_own]
    enc_own = [line_end(enc_lines[order.index(i)], chunk) for i in range(len(order))]
    enc_got = [lax.ppermute(share, "pipe", [(1, 0)]) for share in enc_own]
    is_first = pipe == 0
    lower = jnp.where(is_first, jnp.concatenate(enc_own, axis=1), jnp.concatenate(dec_got, axis=1))
    upper = jnp.where(is_first, jnp.concatenate(enc_got, axis=1), jnp.concatenate(dec_own, axis=1))
    region_grad = jnp.transpose(jnp.concatenate([lower, upper[:, overlap:]], axis=1))[None]

    sums = after(sums, *joined, *dec_got, *[line[0] for line in enc_lines[:-1]])
    for bit in exchange_bits("dp"):
        sums = exchanged(sums, "dp", bit)
    lower, upper = join_cores(sums)
    bias_grad = jnp.concatenate([lower[pack_half:].reshape(-1), upper[pack_half:].reshape(-1)[overlap:]])
    lower, upper = lower[:pack_half], upper[:pack_half]

    shapes = [w.shape for w in enc + dec]
    ranked = ordered([RankedShape(*shape, index) for index, shape in enumerate(shapes)])
    rows_of = {entry.index: row for row, entry in zip(places, ranked)}
    groups = [(0,), (1,), (2,), (3, 4), (5,), (6,), (7, 8), (9,), (10,), (11,)]
    cuts = [[(rows_of[i], *shapes[i]) for i in group] for group in groups] + [[(pack_rows - 1, 1, 1)]]
    out_shape = [jax.ShapeDtypeStruct((sum(c[1] for c in cut), cut[0][2]), jnp.float32) for cut in cuts]
    (d_bias_in, d_square, d_bias_two, d_heads, d_mean_b, d_var_b, d_first, d_bias_one, d_dec_square, d_dec_bias_two,
     loss_total) = one_step(
        functools.partial(unpack_kernel, cuts), [lower, upper], out_shape, "unpack", None,
        [pltpu.VMEM((pack_rows, width), jnp.float32)],
    )
    mean_loss = loss_total[0, 0] / (cell_total * region_total)
    return (
        region_grad,
        bias_grad,
        d_bias_in[0],
        d_square,
        d_bias_two[0],
        jnp.transpose(d_heads),
        jnp.concatenate([d_mean_b[0], d_var_b[0]], axis=0),
        d_first,
        d_bias_one[0],
        d_dec_square,
        d_dec_bias_two[0],
        mean_loss,
    )


def solution(mesh):
    in_specs = (
        P("dp", "tensor"),
        P("pipe", "tensor", None),
        P("tensor"),
        P("tensor"),
        P("tensor"),
        P("dp"),
        P("dp"),
        P("dp", None),
        *[P()] * 9,
    )
    out_specs = (P("pipe", "tensor", "dp"), P("tensor"), *[P()] * 10)
    return jax.shard_map(body, mesh=mesh, in_specs=in_specs, out_specs=out_specs, check_vma=False)
```

```python
import functools

import jax
import jax.numpy as jnp
import numpy as np
from jax import lax
from jax.experimental import pallas as pl
from jax.experimental.pallas import tpu as pltpu
from jax.sharding import PartitionSpec as P

EXACT = lax.Precision.HIGHEST
NORM_EPS = 1e-05
LOG2E = float(np.log2(np.e))
LN2 = float(np.log(2.0))
BIG_BITS = 56
BIG = float(2.0**BIG_BITS)
MIB = 1 << 20


def params_of(mib):
    return pltpu.CompilerParams(vmem_limit_bytes=mib * MIB)


def layer_norm(values):
    centred = values - jnp.mean(values, axis=-1, keepdims=True)
    return centred * lax.rsqrt(jnp.mean(centred * centred, axis=-1, keepdims=True) + NORM_EPS)


def silu(values):
    return values * jax.nn.sigmoid(values)


def mm(a, b):
    return lax.dot_general(a, b, (((1,), (0,)), ((), ())), precision=EXACT, preferred_element_type=jnp.float32)


def mm_t(a, b):
    return lax.dot_general(a, b, (((1,), (1,)), ((), ())), precision=EXACT, preferred_element_type=jnp.float32)


def encoder_small(summed, bias_in, square, bias_two, mean_w, var_w, mean_b, var_b, noise_rows):
    hidden = silu(layer_norm(summed + bias_in))
    hidden = silu(layer_norm(mm(hidden, square) + bias_two))
    average = mm_t(hidden, mean_w) + mean_b
    variance = jnp.exp(mm_t(hidden, var_w) + var_b) + 0.0001
    sample = average + jnp.sqrt(variance) * noise_rows
    kl_rows = 0.5 * jnp.sum(average * average + variance - jnp.log(variance) - 1.0, axis=1, keepdims=True)
    return (sample, jnp.sum(kl_rows, axis=0, keepdims=True))


def decoder_small(latent_rows, onehot, first_z, first_b, bias_one, square, bias_two):
    hidden = silu(layer_norm(mm(latent_rows, first_z) + mm(onehot, first_b) + bias_one))
    return silu(layer_norm(mm(hidden, square) + bias_two))


def onehot_of(ids, width):
    codes = lax.broadcasted_iota(jnp.int32, (ids.shape[0], width), 1)
    return (ids == codes).astype(jnp.float32)


def forward_kernel(count, *refs):
    parts = refs[:count]
    noise, ids = refs[count : count + 2]
    enc = [r[...] for r in refs[count + 2 : count + 9]]
    dec = [r[...] for r in refs[count + 9 : count + 14]]
    summed_out, z_out, g2_out, kl_out = refs[count + 14 :]
    summed = parts[0][...]
    for part in parts[1:]:
        summed = summed + part[...]
    sample, kl_sum = encoder_small(summed, *enc, noise[...])
    z_low = sample.astype(jnp.bfloat16)
    hidden = decoder_small(z_low.astype(jnp.float32), onehot_of(ids[...], dec[1].shape[0]), *dec)
    summed_out[...] = summed
    z_out[...] = z_low
    g2_out[...] = hidden.astype(jnp.bfloat16)
    kl_out[...] = kl_sum


def pack_places(shapes):
    places, row = [], 0
    for rows, _ in shapes:
        places.append(row)
        row += rows if rows == 1 else -(-rows // 8) * 8
    return places, -(-(row + 1) // 16) * 16


def backward_kernel(count, norm_scale, calls, *refs):
    parts = refs[:count]
    summed, z_low, noise, ids = refs[count : count + 4]
    enc = [r[...] for r in refs[count + 4 : count + 11]]
    dec = [r[...] for r in refs[count + 11 : count + 16]]
    owed = refs[count + 16]
    losses = refs[count + 17 : count + 17 + calls]
    dp_out, pack_out = refs[count + 17 + calls :]
    dg2 = parts[0][...]
    for part in parts[1:]:
        dg2 = dg2 + part[...]
    onehot = onehot_of(ids[...], dec[1].shape[0])
    unused, pull = jax.vjp(lambda z, *w: decoder_small(z, onehot, *w), z_low[...].astype(jnp.float32), *dec)
    dz, *dec_grads = pull(dg2)
    noise_rows = noise[...]
    unused, pull = jax.vjp(lambda s, *w: encoder_small(s, *w, noise_rows), summed[...], *enc)
    dz_low = dz.astype(jnp.bfloat16).astype(jnp.float32)
    dp, *enc_grads = pull((dz_low, jnp.full((1, 1), norm_scale, jnp.float32)))
    dp_out[...] = dp.astype(jnp.bfloat16)
    pack_out[...] = jnp.zeros_like(pack_out)
    grads = ordered(enc_grads + dec_grads)
    for row, grad in zip(pack_places([g.shape for g in grads])[0], grads):
        pack_out[row : row + grad.shape[0], : grad.shape[1]] = grad
    loss = losses[0][...]
    for ref in losses[1:]:
        loss = loss + ref[...]
    loss = jnp.sum(jnp.sum(loss, axis=0, keepdims=True), axis=1, keepdims=True) * (LN2 / norm_scale) + owed[...]
    pack_out[pack_out.shape[0] - 1 :, 0:1] = loss


def unpack_kernel(cuts, lower_ref, upper_ref, *refs):
    pack = refs[-1]
    half = lower_ref.shape[0]
    pack[:half, :] = lower_ref[...]
    pack[half:, :] = upper_ref[...]
    for cut, out in zip(cuts, refs[:-1]):
        at = 0
        for row, rows, columns in cut:
            out[at : at + rows, :] = pack[row : row + rows, :columns]
            at += rows


class RankedShape:
    def __init__(self, rows, columns, index):
        self.shape, self.index = (rows, columns), index


def ordered(values):
    return [v for v in values if v.shape[0] > 1] + [v for v in values if v.shape[0] == 1]


STRIP = 16
TOP = 32767.0


def coded_rows(share, chunk):
    return chunk // 256 * share + STRIP


def code(values, out_ref, base, tile, share, strip):
    largest = jnp.maximum(jnp.max(jnp.abs(values), axis=0, keepdims=True), 1e-30)
    level = jnp.ceil(jnp.log2(largest) * 64.0 + 0.01)
    scaled = values * (TOP * jnp.exp2(level * (-1.0 / 64.0)))
    at = base + tile * share
    out_ref[at : at + share, :] = jnp.floor(scaled + 0.5).astype(jnp.int32).astype(jnp.int16)
    row = lax.broadcasted_iota(jnp.int32, (STRIP, 256), 0)
    return jnp.where(row == tile, level, strip)


def code_all(parts, out_ref, base, share):
    strip = jnp.zeros((STRIP, 256), jnp.float32)
    for tile, values in enumerate(parts):
        strip = code(values, out_ref, base, tile, share, strip)
    at = base + len(parts) * share
    out_ref[at : at + STRIP, :] = strip.astype(jnp.int32).astype(jnp.int16)


def decode(in_ref, base, tiles, share, tile):
    at = base + tiles * share
    level = in_ref[at : at + STRIP, :].astype(jnp.int32).astype(jnp.float32)[tile : tile + 1, :]
    at = base + tile * share
    values = in_ref[at : at + share, :].astype(jnp.int32).astype(jnp.float32)
    return values * (jnp.exp2(level * (1.0 / 64.0)) * (1.0 / TOP))


def give_shares(z, dw_ref, sent_ref, own_ref, other_ref):
    share, chunk = own_ref.shape

    def rows(which):
        return pl.ds(pl.multiple_of(which * share, 16), share)

    for place, which in enumerate((z ^ 1, z ^ 3)):
        parts = [dw_ref[rows(which), c : c + 256] for c in range(0, chunk, 256)]
        code_all(parts, sent_ref, place * coded_rows(share, chunk), share)
    own_ref[...] = dw_ref[rows(z), :]
    other_ref[...] = dw_ref[rows(z ^ 2), :]


def share_outputs(width, chunk, count, coded):
    if not coded:
        return [pl.BlockSpec((width, chunk), lambda j, h: (0, j))], [jax.ShapeDtypeStruct((width, count * chunk), jnp.float32)]
    share = width // 4
    rows = 2 * coded_rows(share, chunk)
    specs = [pl.BlockSpec((rows, 256), lambda j, h: (j, 0))] + [pl.BlockSpec((share, chunk), lambda j, h: (0, j))] * 2
    shapes = [jax.ShapeDtypeStruct((count * rows, 256), jnp.int16)]
    return specs, shapes + [jax.ShapeDtypeStruct((share, count * chunk), jnp.float32)] * 2


def join_kernel(got_ref, own_ref, other_ref, sent_ref, sum_ref, *, chunk):
    share, width = own_ref.shape
    tiles, rows = chunk // 256, coded_rows(share, chunk)
    for j in range(width // chunk):
        parts = []
        for tile in range(tiles):
            cols = slice(j * chunk + tile * 256, j * chunk + tile * 256 + 256)
            sum_ref[:, cols] = own_ref[:, cols] + decode(got_ref, 2 * j * rows, tiles, share, tile)
            parts.append(other_ref[:, cols] + decode(got_ref, (2 * j + 1) * rows, tiles, share, tile))
        code_all(parts, sent_ref, j * rows, share)


def total_kernel(sum_ref, got_ref, out_ref, *, chunk):
    share, width = sum_ref.shape
    tiles, rows = chunk // 256, coded_rows(share, chunk)
    for j in range(width // chunk):
        for tile in range(tiles):
            cols = slice(j * chunk + tile * 256, j * chunk + tile * 256 + 256)
            out_ref[:, cols] = sum_ref[:, cols] + decode(got_ref, j * rows, tiles, share, tile)


def one_step(kernel, args, out_shape, name, place=None, scratch=()):
    def whole(array):
        return pl.BlockSpec(array.shape, lambda i, rank=len(array.shape): (0,) * rank)

    front = [] if place is None else [place]
    return pl.pallas_call(
        kernel,
        grid=(1,),
        in_specs=[pl.BlockSpec(memory_space=pltpu.SMEM)] * len(front) + [whole(x) for x in args],
        out_specs=[whole(x) for x in out_shape],
        out_shape=list(out_shape),
        scratch_shapes=list(scratch),
        compiler_params=params_of(48),
        name=name,
    )(*front, *args)


def line_start(pieces):
    if len(pieces) == 1:
        return [lax.psum_scatter(pieces[0], "dp", scatter_dimension=0, tiled=True)]
    return [lax.ppermute(pieces[0], "dp", [(i, i ^ 1) for i in range(4)]), *pieces[1:]]


def line_joined(state, chunk):
    if len(state) == 1:
        return state
    got, own, other = state
    sent = jax.ShapeDtypeStruct((got.shape[0] // 2, 256), jnp.int16)
    kernel = functools.partial(join_kernel, chunk=chunk)
    return one_step(kernel, state, [sent, jax.ShapeDtypeStruct(own.shape, jnp.float32)], "join")


def line_last(state):
    if len(state) == 1:
        return state
    return [lax.ppermute(state[0], "dp", [(i, i ^ 2) for i in range(4)]), state[1]]


def line_end(state, chunk):
    if len(state) == 1:
        return state[0]
    got, own = state
    kernel = functools.partial(total_kernel, chunk=chunk)
    return one_step(kernel, [own, got], [jax.ShapeDtypeStruct(own.shape, jnp.float32)], "total")[0]


def after(value, *others):
    return lax.optimization_barrier((value, *others))[0]


def chosen(core, encoder, kept_ref, got_ref):
    own = core == (0 if encoder else 1)
    return jnp.where(own, kept_ref[...], got_ref[...])


def weight_specs(chunk, width, per_half, first, got_first, encoder):
    owner = 0 if encoder else 1

    def kept(j, h):
        return (jnp.where(h[1] == owner, h[0] * per_half + first + j, 0), 0)

    def got(j, h):
        return (jnp.where(h[1] == owner, 0, got_first + j), 0)

    return [pl.BlockSpec((chunk, width), kept), pl.BlockSpec((chunk, width), got)]


def project_kernel(started, half_ref, x_ref, kept_ref, got_ref, bias_ref, factor_ref, keep_ref, *refs):
    out_ref, seen_ref = refs[-2:]
    chunk, width = kept_ref.shape
    keep = keep_ref[...]
    row = lax.broadcasted_iota(jnp.int32, (width, chunk), 0)
    terms = jnp.where(row == 0, keep, 0.0)
    rest = keep * (bias_ref[...] + jnp.log(factor_ref[...]))
    for place in range(1, 4):
        high = rest.astype(jnp.bfloat16).astype(jnp.float32)
        terms = jnp.where(row == place, high, terms)
        rest = rest - high
    right = jnp.concatenate([chosen(half_ref[1], True, kept_ref, got_ref), jnp.transpose(terms).astype(jnp.bfloat16)], axis=1)
    part = jnp.dot(x_ref[...], right, preferred_element_type=jnp.float32)

    @pl.when(pl.program_id(0) == 0)
    def first():
        out_ref[...] = part[:, :width] + refs[0][...] if started else part[:, :width]
        seen_ref[...] = part[:, width:] + refs[1][...] if started else part[:, width:]

    @pl.when(pl.program_id(0) != 0)
    def later():
        out_ref[...] += part[:, :width]
        seen_ref[...] += part[:, width:]


def project(half, peaks, kept, got, region_rows, before, first, got_first, count, chunk, per_half):
    cells, width = peaks.shape[0], kept.shape[1]
    whole = pl.BlockSpec((cells, width), lambda j, h: (0, 0))
    row = pl.BlockSpec((1, chunk), lambda j, h: (0, h[0] * per_half + first + j))
    return pl.pallas_call(
        functools.partial(project_kernel, bool(before)),
        grid_spec=pltpu.PrefetchScalarGridSpec(
            num_scalar_prefetch=1,
            grid=(count,),
            in_specs=[
                pl.BlockSpec((cells, chunk), lambda j, h: (0, h[0] * per_half + first + j)),
                *weight_specs(chunk, width, per_half, first, got_first, True),
                row,
                row,
                row,
            ]
            + [whole] * len(before),
            out_specs=[whole, whole],
        ),
        out_shape=[jax.ShapeDtypeStruct((cells, width), jnp.float32)] * 2,
        compiler_params=params_of(48),
        cost_estimate=pl.CostEstimate(
            flops=2 * cells * count * chunk * width, bytes_accessed=2 * cells * count * chunk, transcendentals=0
        ),
        name="project",
    )(half, peaks, kept, got, *region_rows, *before)


def regions_kernel(
    tile, rows_at_once, piece, norm_scale, cut, started, coded, half_ref, x_ref, kept_ref, got_ref, rest_ref, g_ref, gt_ref, bias_in_ref, factor_ref, keep_ref,
    cf_ref, *refs,
):
    outs = refs[1 if started else 0 :]
    dg_ref, bias_ref, loss_ref = outs[:3]
    m0, m1, e0, e1, w_ref, dw_ref = outs[-6:] if coded else (*outs[4:], outs[3])
    cells, chunk = x_ref.shape
    blocks = cells // rows_at_once
    M, E = (m0, m1), (e0, e1)

    got = jnp.where(pl.program_id(0) < cut, got_ref[...], rest_ref[...])
    w_ref[...] = jnp.where(half_ref[1] == 1, kept_ref[...], got)

    @pl.when(pl.program_id(0) == 0)
    def first():
        dg_ref[...] = refs[0][...] if started else jnp.zeros_like(dg_ref)
        loss_ref[...] = jnp.zeros_like(loss_ref)

    def one_tile(t, carry):
        cols = pl.ds(pl.multiple_of(t * tile, 128), tile)
        w = w_ref[cols, :]
        w2 = jnp.concatenate([w, w], axis=1)
        wide = (8, tile)
        bias_row = jnp.exp(bias_in_ref[:, cols])
        a = jnp.broadcast_to(bias_row, wide)[None]
        fa = jnp.broadcast_to(bias_row * factor_ref[:, cols], wide)[None]
        ck = jnp.broadcast_to(keep_ref[:, cols] * norm_scale, wide)[None]

        def rows(i, o=0, n=rows_at_once):
            return pl.ds(pl.multiple_of(i * rows_at_once + o, 16), n)

        def logit(i, s, o, n):
            M[s][o : o + n, :] = lax.dot_general(
                g_ref[rows(i, o, n), :], w2, (((1,), (1,)), ((), ())), preferred_element_type=jnp.float32
            )

        def elementwise(i, s, o, sums):
            e_sum, l_sum = sums
            shape = (piece // 8, 8, tile)
            u = jnp.exp2(M[s][o : o + piece, :]).reshape(shape)
            cf = cf_ref[rows(i, o, piece), :]
            cf = jnp.concatenate([cf] * (tile // 128), axis=1).reshape(shape)
            seen = (x_ref[rows(i, o, piece), cols] * jnp.bfloat16(BIG)).astype(jnp.float32).reshape(shape)
            total = u + a
            rest = (total - fa * cf) + seen
            d = pltpu.reciprocal(rest, approx=True)
            slope = (u * ck) * (d - pltpu.reciprocal(total, approx=True))
            ratio = (d * total).reshape(piece // 16, 2, 8, tile)
            E[s][o : o + piece, :] = slope.reshape(piece, tile).astype(jnp.bfloat16)
            e_sum = e_sum + jnp.sum(slope, axis=0)
            l_sum = l_sum + jnp.sum(jnp.log2(ratio[:, 0] * ratio[:, 1]), axis=0)
            return e_sum, l_sum

        def cell_grad(i, s):
            dg_ref[rows(i), :] += jnp.dot(E[s][...], w, preferred_element_type=jnp.float32)

        def region_grad(i, s, start=False):
            part = jnp.dot(gt_ref[i], E[s][...], preferred_element_type=jnp.float32)
            if start:
                dw_ref[:, cols] = part
            else:
                dw_ref[:, cols] += part

        def step(i, s, sums, logits=True, grads=True, start=False):
            if logits:
                logit(i + 1, 1 - s, 0, rows_at_once)
            for o in range(0, rows_at_once, piece):
                sums = elementwise(i, s, o, sums)
                if grads and o == rows_at_once // 2:
                    cell_grad(i - 1, 1 - s)
            if grads:
                region_grad(i - 1, 1 - s, start)
            return sums

        zero = jnp.zeros(wide, jnp.float32)
        sums = (zero, zero)
        logit(0, 0, 0, rows_at_once)
        sums = step(0, 0, sums, grads=False)
        for i in range(1, blocks):
            sums = step(i, i % 2, sums, logits=i < blocks - 1, start=i == 1)
        cell_grad(blocks - 1, (blocks - 1) % 2)
        region_grad(blocks - 1, (blocks - 1) % 2, blocks == 1)
        bias_ref[:, cols] = jnp.sum(sums[0], axis=0, keepdims=True)
        kept = sums[1] * ck[0]
        for c in range(0, tile, 128):
            loss_ref[...] += kept[:, c : c + 128]
        return carry

    lax.fori_loop(0, chunk // tile, one_tile, 0)
    if coded:
        give_shares(half_ref[2], dw_ref, *outs[3:6])


def regions_pass(norm_scale, half, peaks, kept, got_pair, hidden, hidden_t, region_rows, cf, before, first, count, chunk, per_half, coded):
    cells, width = peaks.shape[0], kept.shape[1]
    blocks, _, rows = hidden_t.shape
    tile, piece = min(256, chunk), 64
    cut = got_pair[0].shape[0] // chunk
    started = before is not None
    whole = pl.BlockSpec((cells, width), lambda j, h: (0, 0))
    row = pl.BlockSpec((1, chunk), lambda j, h: (0, h[0] * per_half + first + j))
    share_specs, share_shapes = share_outputs(width, chunk, count, coded)
    return pl.pallas_call(
        functools.partial(regions_kernel, tile, rows, piece, norm_scale, cut - first, started, coded),
        grid_spec=pltpu.PrefetchScalarGridSpec(
            num_scalar_prefetch=1,
            grid=(count,),
            in_specs=[
                pl.BlockSpec((cells, chunk), lambda j, h: (0, h[0] * per_half + first + j)),
                *weight_specs(chunk, width, per_half, first, first, False)[:1],
                pl.BlockSpec((chunk, width), lambda j, h: (jnp.where(h[1] == 1, 0, jnp.minimum(first + j, cut - 1)), 0)),
                pl.BlockSpec((chunk, width), lambda j, h: (jnp.where(h[1] == 1, 0, jnp.maximum(first + j - cut, 0)), 0)),
                pl.BlockSpec((cells, 2 * width), lambda j, h: (0, 0)),
                pl.BlockSpec((blocks, width, rows), lambda j, h: (0, 0, 0)),
                row, row, row, whole,
            ]
            + [whole] * started,
            out_specs=[
                whole,
                pl.BlockSpec((1, chunk), lambda j, h: (0, j)),
                pl.BlockSpec((8, 128), lambda j, h: (0, 0)),
                *share_specs,
            ],
            scratch_shapes=[pltpu.VMEM((rows, tile), jnp.float32)] * 2
            + [pltpu.VMEM((rows, tile), jnp.bfloat16)] * 2
            + [pltpu.VMEM((chunk, width), jnp.bfloat16)]
            + [pltpu.VMEM((width, chunk), jnp.float32)] * coded,
        ),
        out_shape=[
            jax.ShapeDtypeStruct((cells, width), jnp.float32),
            jax.ShapeDtypeStruct((1, count * chunk), jnp.float32),
            jax.ShapeDtypeStruct((8, 128), jnp.float32),
            *share_shapes,
        ],
        compiler_params=params_of(56),
        cost_estimate=pl.CostEstimate(
            flops=10 * cells * count * chunk * width,
            bytes_accessed=2 * cells * count * chunk,
            transcendentals=16 * cells * count * chunk,
        ),
        name="regions",
    )(half, peaks, kept, *got_pair, hidden, hidden_t, *region_rows, cf, *([before] if started else []))


def outer_kernel(coded, half_ref, x_ref, left_ref, *outs):
    dw_ref = outs[-1]
    tile = min(256, x_ref.shape[1])
    for c in range(0, x_ref.shape[1], tile):
        cols = slice(c, c + tile)
        dw_ref[:, cols] = jnp.dot(left_ref[...], x_ref[:, cols], preferred_element_type=jnp.float32)
    if coded:
        give_shares(half_ref[2], dw_ref, *outs[:3])


def outer(half, peaks, left, first, count, chunk, per_half, coded):
    width, cells = left.shape
    share_specs, share_shapes = share_outputs(width, chunk, count, coded)
    return pl.pallas_call(
        functools.partial(outer_kernel, coded),
        grid_spec=pltpu.PrefetchScalarGridSpec(
            num_scalar_prefetch=1,
            grid=(count,),
            in_specs=[
                pl.BlockSpec((cells, chunk), lambda j, h: (0, h[0] * per_half + first + j)),
                pl.BlockSpec((width, cells), lambda j, h: (0, 0)),
            ],
            out_specs=share_specs,
            scratch_shapes=[pltpu.VMEM((width, chunk), jnp.float32)] * coded,
        ),
        out_shape=share_shapes,
        compiler_params=params_of(48),
        cost_estimate=pl.CostEstimate(
            flops=2 * cells * count * chunk * width, bytes_accessed=2 * cells * count * chunk, transcendentals=0
        ),
        name="outer",
    )(half, peaks, left)


def part_of(values, which, size, axis=0):
    return lax.dynamic_slice_in_dim(values, which * size, size, axis)


def across_cores(values):
    return lax.ppermute(values, "pipe", [(0, 1), (1, 0)])


def shift_of(step, index, count):
    if count & (count - 1) == 0:
        return index ^ step
    return (index + step) % count


def scatter_cells(partial):
    cells = partial.shape[0]
    pipe, mine, count = lax.axis_index("pipe"), lax.axis_index("tensor"), lax.axis_size("tensor")
    half = cells // 2
    got = across_cores(part_of(partial, 1 - pipe, half))
    chip_sum = part_of(partial, pipe, half) + got
    rows = half // count
    pieces = [part_of(chip_sum, mine, rows)]
    for step in range(1, count):
        there = shift_of(step, mine, count)
        route = [(i, shift_of(step, i, count)) for i in range(count)]
        pieces.append(lax.ppermute(part_of(chip_sum, there, rows), "tensor", route))
    return pieces


def gather_cells(own):
    count = lax.axis_size("tensor")
    pieces = [own]
    for step in range(1, count):
        route = [(i, shift_of(step, i, count)) for i in range(count)]
        pieces.append(lax.ppermute(own, "tensor", route))
    return pieces + [across_cores(piece) for piece in pieces]


def rows_at(place_ref, index, count, rows):
    core, mine = place_ref[0], place_ref[1]
    step = index % count
    if count & (count - 1) == 0:
        sender = mine ^ step
    else:
        sender = lax.rem(mine - step + count, jnp.int32(count))
    here = core if index < count else 1 - core
    return (here * count + sender) * rows


def hidden_kernel(count, place_ref, *refs):
    pieces, (wide_ref, turned_ref, all_s) = refs[:-3], refs[-3:]
    rows, width = pieces[0].shape
    for index, piece in enumerate(pieces):
        at = pl.ds(pl.multiple_of(rows_at(place_ref, index, count, rows), 16), rows)
        all_s[at, :] = piece[...].astype(jnp.float32)
    scaled = all_s[...] * (-LOG2E)
    high = scaled.astype(jnp.bfloat16)
    wide_ref[:, :width] = high
    wide_ref[:, width:] = (scaled - high.astype(jnp.float32)).astype(jnp.bfloat16)
    size = turned_ref.shape[2]
    for block in range(turned_ref.shape[0]):
        turned_ref[block] = jnp.transpose(all_s[block * size : (block + 1) * size, :]).astype(jnp.bfloat16)


def left_kernel(count, place_ref, *refs):
    pieces, (left_ref, all_s) = refs[:-2], refs[-2:]
    rows = pieces[0].shape[0]
    for index, piece in enumerate(pieces):
        at = pl.ds(pl.multiple_of(rows_at(place_ref, index, count, rows), 16), rows)
        all_s[at, :] = piece[...].astype(jnp.float32)
    left_ref[...] = jnp.transpose(all_s[...]).astype(jnp.bfloat16)


def assemble(kernel, place, pieces, out_shape, name):
    rows, width = pieces[0].shape
    return one_step(
        functools.partial(kernel, len(pieces) // 2), pieces, out_shape, name, place,
        [pltpu.VMEM((rows * len(pieces), width), jnp.float32)],
    )


def exchange_bits(axis):
    count = lax.axis_size(axis)
    return [1 << i for i in range((count - 1).bit_length())]


def exchanged(values, axis, bit):
    count = lax.axis_size(axis)
    return values + lax.ppermute(values, axis, [(i, i ^ bit) for i in range(count)])


def all_sum(values, axes):
    for axis in axes:
        for bit in exchange_bits(axis):
            values = exchanged(values, axis, bit)
    return values


def join_cores(own):
    other = across_cores(own)
    first = lax.axis_index("pipe") == 0
    return jnp.where(first, own, other), jnp.where(first, other, own)


def body(
    peak_data,
    region_weights,
    out_bias,
    region_factor,
    region_keep,
    cell_factor,
    batch_ids,
    latent_noise,
    enc_bias_in,
    enc_square,
    enc_bias_two,
    enc_heads,
    head_bias,
    dec_first,
    dec_bias_one,
    dec_square,
    dec_bias_two,
):
    cells, regions_local = peak_data.shape
    weight = region_weights[0]
    width = weight.shape[1]
    latent = latent_noise.shape[1]
    batches = dec_first.shape[0] - latent
    window = -(-regions_local // 256) * 128
    overlap = 2 * window - regions_local
    pipe, mine, tensors = lax.axis_index("pipe"), lax.axis_index("tensor"), lax.axis_size("tensor")
    cell_total = cells * lax.axis_size("dp")
    region_total = regions_local * tensors
    norm_scale = float(cell_total) ** (-0.5)

    def of_core(values, core, axis=0):
        return lax.dynamic_slice_in_dim(values, core * (regions_local - window), window, axis)

    region_rows = [out_bias, region_factor, region_keep.astype(jnp.float32)]
    dp_at = lax.axis_index("dp")
    place = jnp.stack([pipe, mine, dp_at]).astype(jnp.int32)
    chunk = next(c for c in (1792, 256, 128) if window % c == 0 and (regions_local - window) % c == 0)
    chunks = window // chunk
    ahead = min(2, chunks - 1) * chunk
    coded = lax.axis_size("dp") == 4 and chunk % 256 == 0
    if overlap:
        mine_alone = (pipe == 0) | (jnp.arange(window) >= overlap)
        region_rows = [of_core(row, pipe) for row in region_rows]
        region_rows[2] = jnp.where(mine_alone, region_rows[2], 0.0)
        peak_data = of_core(peak_data, pipe, 1)
        own = of_core(weight, pipe)
        got = across_cores(of_core(weight, 1 - pipe))
        kept_enc = got_enc = jnp.where(mine_alone[:, None], jnp.where(pipe == 0, own, got), 0)
        weight = jnp.where(pipe == 0, got, own)
        got_pair, got_spans = (weight, weight), [(0, chunks)]
        got_parts = [(kept_enc, got_enc, 0, 0, chunks)]
        half = jnp.stack([jnp.zeros_like(place[0]), place[0], place[2]])
    else:
        other_at = (1 - pipe) * (regions_local - window)
        got_first = across_cores(lax.dynamic_slice_in_dim(weight, other_at, ahead, 0))
        got_rest = across_cores(lax.dynamic_slice_in_dim(weight, other_at + ahead, window - ahead, 0))
        got_parts = [(weight, got_first, 0, 0, ahead // chunk), (weight, got_rest, ahead // chunk, 0, chunks - ahead // chunk)]
        cut = ahead // chunk
        most = -(-chunks * 4 // 7)
        got_pair, got_spans = (got_first, got_rest), [(0, most), (most, chunks)]
        half = jnp.stack([place[0], place[0], place[2]])

    own_rows = cells // (2 * tensors)
    own_at = pipe * tensors + mine
    noise_own = part_of(latent_noise, own_at, own_rows)
    ids_own = part_of(batch_ids[:, None], own_at, own_rows)
    heads_t = jnp.transpose(enc_heads)
    enc = (
        enc_bias_in[None], enc_square, enc_bias_two[None], heads_t[:latent], heads_t[latent:],
        head_bias[None, :latent], head_bias[None, latent:],
    )
    dec = (dec_first[:latent], dec_first[latent:], dec_bias_one[None], dec_square, dec_bias_two[None])

    region_rows = [row[None] for row in region_rows]
    cf_wide = jnp.broadcast_to(cell_factor[:, None], (cells, 128))
    partial = []
    for kept_w, got_w, first, at, count in got_parts:
        partial = project(half, peak_data, kept_w, got_w, region_rows, partial, first, at, count, chunk, chunks)
    partial, seen = partial
    pieces = scatter_cells(partial)
    owed = jnp.sum(seen[:, 0] * (BIG_BITS * LN2 - jnp.log(cell_factor))) - jnp.sum(seen[:, 1:4])
    early = (noise_own, ids_own, enc, dec, cf_wide, owed[None, None])
    pieces, early = lax.optimization_barrier((pieces, early))
    noise_own, ids_own, enc, dec, cf_wide, owed = early
    summed, z_low, g2_own, kl_sum = one_step(
        functools.partial(forward_kernel, len(pieces)),
        [*pieces, noise_own, ids_own, *enc, *dec],
        [
            jax.ShapeDtypeStruct((own_rows, width), jnp.float32),
            jax.ShapeDtypeStruct((own_rows, latent), jnp.bfloat16),
            jax.ShapeDtypeStruct((own_rows, width), jnp.bfloat16),
            jax.ShapeDtypeStruct((1, 1), jnp.float32),
        ],
        "small_forward",
    )
    rows_b = min(512, cells // 2)
    hidden, hidden_t = assemble(
        hidden_kernel, place, gather_cells(g2_own),
        [
            jax.ShapeDtypeStruct((cells, 2 * width), jnp.bfloat16),
            jax.ShapeDtypeStruct((cells // rows_b, width, rows_b), jnp.bfloat16),
        ],
        "hidden",
    )

    dg2, lines, biases, losses = None, [], [], []
    for first, end in got_spans:
        if len(lines) > 1:
            lines[-2] = line_joined(lines[-2], chunk)
            dg2 = after(dg2, lines[-2][0])
            lines[-2] = line_last(lines[-2])
        dg2, bias, loss, *shares = regions_pass(
            norm_scale, half, peak_data, weight, got_pair, hidden, hidden_t, region_rows, cf_wide, dg2, first,
            end - first, chunk, chunks, coded,
        )
        dg2 = after(dg2, *[line[0] for line in lines])
        lines.append(line_start(shares))
        biases.append(bias)
        losses.append(loss)
    pieces = scatter_cells(dg2)
    if len(lines) > 1:
        lines[-2] = line_joined(lines[-2], chunk)
        pieces[0] = after(pieces[0], lines[-2][0])
        lines[-2] = line_last(lines[-2])
    grad_shapes = [w.shape for w in ordered(enc + dec)]
    places, pack_rows = pack_places(grad_shapes)
    pack_half = pack_rows // 2
    dp_own, pack = one_step(
        functools.partial(backward_kernel, len(pieces), norm_scale, len(losses)),
        [*pieces, summed, z_low, noise_own, ids_own, *enc, *dec, kl_sum + owed, *losses],
        [
            jax.ShapeDtypeStruct((own_rows, width), jnp.bfloat16),
            jax.ShapeDtypeStruct((pack_rows, width), jnp.float32),
        ],
        "small_backward",
    )
    gathered = gather_cells(dp_own)
    lines[-1][0] = after(lines[-1][0], *gathered)
    lines[-1] = line_joined(lines[-1], chunk)
    (left,) = assemble(left_kernel, place, gathered, [jax.ShapeDtypeStruct((width, cells), jnp.bfloat16)], "left")
    left = after(left, *[line[0] for line in lines])
    lines[-1] = line_last(lines[-1])

    first, second = max(1, chunks * 2 // 7), max(2, chunks * 5 // 7)
    spans = [(0, first), (first, second), (second, chunks)] if chunks > 2 else [(0, chunks)]
    order = list(range(len(spans)))
    enc_lines, under_way = [], []
    for index, (first, end) in enumerate([spans[i] for i in order]):
        if index:
            left = after(left, shares[0], *([lines[-1][0]] if index == 1 else []))
        if index > 1:
            line = line_joined(under_way.pop(0), chunk)
            left = after(left, line[0])
            enc_lines.append(line_last(line))
        shares = list(outer(half, peak_data, left, first, end - first, chunk, chunks, coded))
        newest = shares[0]
        beside = [line[0] for line in under_way + enc_lines]
        shares[0] = after(shares[0], *beside)
        under_way.append(line_start(shares))
    joined, newest_got = [], under_way[-1][0]
    for line in under_way:
        line[0] = after(line[0], newest)
        line = line_joined(line, chunk)
        joined.append(line[0])
        enc_lines.append(line_last(line))

    pack, *ends = lax.optimization_barrier((after(pack, joined[0]), *[line[0] for line in lines]))
    lines = [[end, *line[1:]] for end, line in zip(ends, lines)]
    pack = part_of(pack, pipe, pack_half) + across_cores(part_of(pack, 1 - pipe, pack_half))
    pack = all_sum(after(pack, newest_got), ["tensor"])
    sums = jnp.concatenate([pack, jnp.concatenate(biases, axis=1).reshape(-1, 128)], axis=0)

    dec_own = [line_end(line, chunk) for line in lines]
    dec_got = [lax.ppermute(share, "pipe", [(0, 1)]) for share in dec_own]
    enc_own = [line_end(enc_lines[order.index(i)], chunk) for i in range(len(order))]
    enc_got = [lax.ppermute(share, "pipe", [(1, 0)]) for share in enc_own]
    is_first = pipe == 0
    lower = jnp.where(is_first, jnp.concatenate(enc_own, axis=1), jnp.concatenate(dec_got, axis=1))
    upper = jnp.where(is_first, jnp.concatenate(enc_got, axis=1), jnp.concatenate(dec_own, axis=1))
    region_grad = jnp.transpose(jnp.concatenate([lower, upper[:, overlap:]], axis=1))[None]

    for bit in exchange_bits("dp"):
        if bit == 1:
            sums = after(sums, *joined, *dec_got, *[line[0] for line in enc_lines[:-1]])
        sums = exchanged(sums, "dp", bit)
    lower, upper = join_cores(sums)
    bias_grad = jnp.concatenate([lower[pack_half:].reshape(-1), upper[pack_half:].reshape(-1)[overlap:]])
    lower, upper = lower[:pack_half], upper[:pack_half]

    shapes = [w.shape for w in enc + dec]
    ranked = ordered([RankedShape(*shape, index) for index, shape in enumerate(shapes)])
    rows_of = {entry.index: row for row, entry in zip(places, ranked)}
    groups = [(0,), (1,), (2,), (3, 4), (5,), (6,), (7, 8), (9,), (10,), (11,)]
    cuts = [[(rows_of[i], *shapes[i]) for i in group] for group in groups] + [[(pack_rows - 1, 1, 1)]]
    out_shape = [jax.ShapeDtypeStruct((sum(c[1] for c in cut), cut[0][2]), jnp.float32) for cut in cuts]
    (d_bias_in, d_square, d_bias_two, d_heads, d_mean_b, d_var_b, d_first, d_bias_one, d_dec_square, d_dec_bias_two,
     loss_total) = one_step(
        functools.partial(unpack_kernel, cuts), [lower, upper], out_shape, "unpack", None,
        [pltpu.VMEM((pack_rows, width), jnp.float32)],
    )
    mean_loss = loss_total[0, 0] / (cell_total * region_total)
    return (
        region_grad,
        bias_grad,
        d_bias_in[0],
        d_square,
        d_bias_two[0],
        jnp.transpose(d_heads),
        jnp.concatenate([d_mean_b[0], d_var_b[0]], axis=0),
        d_first,
        d_bias_one[0],
        d_dec_square,
        d_dec_bias_two[0],
        mean_loss,
    )


def solution(mesh):
    in_specs = (
        P("dp", "tensor"),
        P("pipe", "tensor", None),
        P("tensor"),
        P("tensor"),
        P("tensor"),
        P("dp"),
        P("dp"),
        P("dp", None),
        *[P()] * 9,
    )
    out_specs = (P("pipe", "tensor", "dp"), P("tensor"), *[P()] * 10)
    return jax.shard_map(body, mesh=mesh, in_specs=in_specs, out_specs=out_specs, check_vma=False)
```
